256 devices in a mesh: gx: 128 (over x, z, y_hi, core), ta: 2 (over y_lo).
Axes of the slice: x: 4, y: 4 (y_hi: 2, y_lo: 2; y = y_hi * 2 + y_lo), z: 8, core: 2. Of those that a mesh axis runs over, the one named last changes fastest.
Arguments:
- samples: bfloat16 [2048, 65536], P('gx', 'ta'), may hold values from -6 to 6
- gains: float32 [2, 2048, 1024], P(None, 'gx'), may hold values from -5 to 5
- slot_inputs: int32 [2048], replicated, may hold values from 0 to 2047, each once
- beam_order: int32 [1024], replicated, may hold values from 0 to 1023, each once
Outputs:
- intensity: float32 [2, 1024, 16384], P('ta', 'gx')
The draws below stay inside these ranges and needn't reach their ends.
Inputs may be any that keep to these rules, and one draw needn't show every extreme that they name: `slot_inputs`: each input appears in exactly one slot. `beam_order`: each beam appears in exactly one slot.
All inputs are finite; a program needn't handle non-finite values.
Results may differ from the reference program's by a relative error of at most 0.0059.
Values may be sent and summed in bfloat16 or wider, within the bound.
No kernel may reach another device: no remote copies, remote signals or barrier semaphores. Data moves between devices by JAX's collectives and lax.ppermute only.
A program may use at most 128 MiB of HBM per device.

```python
import math
import jax
import jax.numpy as jnp
from jax import lax

CHANNELS = 1024
FEEDS = 256
CYL = 4
POLS = 2
TAPS = 4
UPCH = 16
FRAME = 2048
INPUTS = 2048
BEAMS = 1024
FRAMES = 32
SAMPLES = 65536
SPECTRA = 2
FINE = 16384


def block_scale(key, extent, split, least, high):
    loudness, own = 1.0, jax.random.fold_in(key, 6)
    for axis_at, blocks in split:
        steps = jnp.exp(jax.random.uniform(jax.random.fold_in(own, axis_at), (blocks,), jnp.float32, least / len(split), high / len(split)))
        loudness = loudness * jnp.repeat(steps, extent[axis_at] // blocks).reshape([-1 if axis == axis_at else 1 for axis in range(len(extent))])
    return loudness


def normal_values(own_key, shape, deviation, reach, pieces=(), kind=jnp.bfloat16):
    drawn = deviation * jax.random.normal(own_key, shape, jnp.float32)
    if pieces:
        drawn = drawn * block_scale(own_key, shape, pieces, -0.22, 0.18)
    return jnp.clip(drawn, -reach, reach).astype(kind)


def setup_inputs(seed: int = 0) -> dict:
    key_of = jax.random.split(jax.random.key(seed), 5)
    return {
        "samples": normal_values(key_of[0], (INPUTS, SAMPLES), 1.0, 6.0, ((0, 128), (1, 2))),
        "gains": normal_values(key_of[1], (2, INPUTS, CHANNELS), 1.0, 5.0, ((1, 128),), jnp.float32),
        "slot_inputs": jax.random.permutation(key_of[2], INPUTS).astype(jnp.int32),
        "beam_order": jax.random.permutation(key_of[3], BEAMS).astype(jnp.int32),
    }


def pfb_window():
    total = TAPS * FRAME
    places = jnp.arange(total, dtype=jnp.float32)
    centred = (places - (total - 1) * 0.5) / FRAME
    hann = 0.5 - 0.5 * jnp.cos(2.0 * math.pi * (places + 0.5) / total)
    window = jnp.sinc(centred) * hann
    window = window * jnp.sqrt(FRAME / jnp.sum(window * window))
    return window.reshape(TAPS, FRAME)

def real_table():
    column = jnp.arange(FRAME, dtype=jnp.int32)
    channel = jnp.arange(CHANNELS, dtype=jnp.int32)
    phase = column[:, None] * channel[None, :] % FRAME
    angle = 2.0 * math.pi / FRAME * phase.astype(jnp.float32)
    scale = 1.0 / math.sqrt(FRAME)
    return (jnp.concatenate([jnp.cos(angle), -jnp.sin(angle)], 1) * scale).astype(jnp.bfloat16)

def complex_table(length):
    index = jnp.arange(length, dtype=jnp.int32)
    phase = index[:, None] * index[None, :] % length
    angle = 2.0 * math.pi / length * phase.astype(jnp.float32)
    scale = 1.0 / math.sqrt(length)
    cosine = jnp.cos(angle) * scale
    sine = jnp.sin(angle) * scale
    table = jnp.stack([jnp.stack([cosine, -sine], 1), jnp.stack([sine, cosine], 1)], 0)
    return table.astype(jnp.bfloat16)

def east_west(real, imag, axis):
    rotations = ((1.0, 0.0), (0.0, -1.0), (-1.0, 0.0), (0.0, 1.0))
    outs_real = []
    outs_imag = []
    for east in range(CYL):
        acc_real = jnp.zeros_like(lax.index_in_dim(real, 0, axis, keepdims=False))
        acc_imag = jnp.zeros_like(acc_real)
        for cyl_index in range(CYL):
            cos_part, sin_part = rotations[east * cyl_index % 4]
            part_real = lax.index_in_dim(real, cyl_index, axis, keepdims=False)
            part_imag = lax.index_in_dim(imag, cyl_index, axis, keepdims=False)
            acc_real = acc_real + part_real * cos_part - part_imag * sin_part
            acc_imag = acc_imag + part_real * sin_part + part_imag * cos_part
        outs_real.append(acc_real * 0.5)
        outs_imag.append(acc_imag * 0.5)
    return (jnp.stack(outs_real, axis), jnp.stack(outs_imag, axis))

def reference(samples, gains, slot_inputs, beam_order):
    window = pfb_window()
    ftable = real_table()
    ntable = complex_table(FEEDS).astype(jnp.float32)
    utable = complex_table(UPCH).astype(jnp.float32)

    def channelize(pair):
        series, gain = pair
        history = jnp.zeros(((TAPS - 1) * FRAME,), jnp.float32)
        padded = jnp.concatenate([history, series.astype(jnp.float32)]).reshape(FRAMES + TAPS - 1, FRAME)
        filtered = padded[0:FRAMES] * window[0]
        for tap in range(1, TAPS):
            filtered = filtered + padded[tap:tap + FRAMES] * window[tap]
        filtered = filtered.astype(jnp.bfloat16)
        spectra = jnp.dot(filtered, ftable, preferred_element_type=jnp.float32)
        spec_real = spectra[:, :CHANNELS]
        spec_imag = spectra[:, CHANNELS:]
        cal_real = gain[0][None, :] * spec_real - gain[1][None, :] * spec_imag
        cal_imag = gain[0][None, :] * spec_imag + gain[1][None, :] * spec_real
        return jnp.stack([cal_real, cal_imag], 1).astype(jnp.bfloat16)
    calibrated = lax.map(channelize, (samples, jnp.transpose(gains, (1, 0, 2))))
    arranged = jnp.take(calibrated, slot_inputs, axis=0)
    by_channel = jnp.transpose(arranged, (3, 0, 1, 2))

    def per_channel(piece):
        piece = piece.reshape(POLS, CYL, FEEDS, FRAMES, 2).astype(jnp.float32)
        north = jnp.einsum('pcnfr,rnsb->fspcb', piece, ntable)
        east_real, east_imag = east_west(north[:, 0], north[:, 1], 2)
        beams = jnp.stack([east_real, east_imag], 1).astype(jnp.bfloat16)
        beams = beams.reshape(FRAMES, 2, POLS, BEAMS)
        beams = jnp.take(beams, beam_order, axis=3)
        beams = beams.reshape(SPECTRA, UPCH, 2, POLS, BEAMS).astype(jnp.float32)
        fine = jnp.einsum('tjrpb,rjsq->tspqb', beams, utable)
        return 0.25 * lax.optimization_barrier(jnp.sum(fine * fine, axis=(1, 2)))
    power = lax.map(per_channel, by_channel)
    return jnp.transpose(power, (1, 3, 0, 2)).reshape(SPECTRA, BEAMS, FINE)
```

```python
import math

import jax
import jax.numpy as jnp
import numpy as np
from jax import lax
from jax.experimental import pallas as pl
from jax.experimental.pallas import tpu as pltpu
from jax.sharding import PartitionSpec as P

CHANNELS = 1024
FRAME = 2 * CHANNELS
HALF = CHANNELS
FEEDS = 256
CYL = 4
POLS = 2
TAPS = 4
UPCH = 16
BEAMS = 1024
INPUTS = 2048
IN_DEV = 16
F_DEV = 16
CH_DEV = 8
BLOCKS = 4
LANES = 128
VMEM_LIMIT = 48 * 1024 * 1024


def from_behind(block, axis, distance):
    devices = range(lax.axis_size(axis))
    route = [(i - distance, i) for i in devices if i - distance in devices]
    return lax.ppermute(block, axis, route)


def pfb_window():
    total = TAPS * FRAME
    places = np.arange(total, dtype=np.float64)
    centred = (places - (total - 1) * 0.5) / FRAME
    hann = 0.5 - 0.5 * np.cos(2.0 * math.pi * (places + 0.5) / total)
    window = np.sinc(centred) * hann
    window = window * np.sqrt(FRAME / np.sum(window * window))
    return window.reshape(TAPS, FRAME).astype(np.float32)


def folded_table():
    n = np.arange(HALF)
    lane = np.arange(LANES)
    out = np.zeros((BLOCKS, 2, HALF, 2 * LANES), np.float32)
    for block in range(BLOCKS):
        for parity in range(2):
            k = 256 * block + 8 * (lane // 4) + 2 * (lane % 4) + parity
            angle = 2.0 * math.pi / FRAME * (n[:, None] * k[None, :] % FRAME)
            out[block, parity, :, :LANES] = np.cos(angle) / math.sqrt(FRAME)
            out[block, parity, :, LANES:] = -np.sin(angle) / math.sqrt(FRAME)
    return out.astype(jnp.bfloat16)


def gain_select():
    lane = np.arange(LANES)
    out = np.zeros((256, 2 * LANES), np.float32)
    for parity in range(2):
        k = 8 * (lane // 4) + 2 * (lane % 4) + parity
        out[k, parity * LANES + lane] = 1.0
    return out.astype(jnp.bfloat16)


def north_table():
    index = np.arange(FEEDS)
    angle = 2.0 * math.pi / FEEDS * (index[:, None] * index[None, :] % FEEDS)
    scale = 1.0 / math.sqrt(FEEDS)
    table = np.concatenate([np.cos(angle), np.sin(angle)], 0) * scale
    return (table.astype(jnp.bfloat16).astype(np.float32) * 0.5).astype(jnp.bfloat16)


def fine_table():
    scale = 1.0 / math.sqrt(UPCH)
    out = np.zeros((2, F_DEV, 2, 4, 2, CH_DEV, UPCH), np.float32)
    j = np.arange(UPCH)
    angle = 2.0 * math.pi / UPCH * (j[:, None] * j[None, :] % UPCH)
    cosine, sine = np.cos(angle) * scale, np.sin(angle) * scale
    for parity in range(2):
        for h in range(4):
            channel = 2 * h + parity
            out[0, :, parity, h, 0, channel, :] = cosine
            out[0, :, parity, h, 1, channel, :] = -sine
            out[1, :, parity, h, 0, channel, :] = sine
            out[1, :, parity, h, 1, channel, :] = cosine
    return out.reshape(256, 256).astype(jnp.bfloat16)


def swap_groups(arrays):
    lane = lax.broadcasted_iota(jnp.int32, arrays[0].shape, 1) // 4
    arrays = list(arrays)
    for bit in (16, 8, 4, 2, 1):
        low = (lane & bit) == 0
        for j in range(32):
            if j & bit:
                continue
            a, b = arrays[j], arrays[j | bit]
            arrays[j] = jnp.where(low, a, pltpu.roll(b, 4 * bit, 1))
            arrays[j | bit] = jnp.where(low, pltpu.roll(a, LANES - 4 * bit, 1), b)
    return arrays


def channelize_kernel(x_ref, prior_ref, w_ref, t_ref, sel_ref, g_ref, out_ref, z_ref):
    block = pl.program_id(0)

    @pl.when(block == 0)
    def _():
        def chunk(c, carry):
            even_odd = []
            for half in range(2):
                at = pl.multiple_of(half * HALF + c * LANES, LANES)
                w = [w_ref[t : t + 1, pl.ds(at, LANES)] for t in range(TAPS)]
                frames = []
                for f in range(TAPS - 1):
                    frames.append(prior_ref[:, pl.ds(f * FRAME + at, LANES)].astype(jnp.float32))
                rows = []
                for f in range(F_DEV):
                    frames.append(x_ref[:, pl.ds(f * FRAME + at, LANES)].astype(jnp.float32))
                    total = frames[f] * w[0]
                    for t in range(1, TAPS):
                        total = total + frames[f + t] * w[t]
                    rows.append(total)
                even_odd.append(rows)
            to = pl.multiple_of(c * LANES, LANES)
            for f in range(F_DEV):
                a, b = even_odd[0][f], even_odd[1][f]
                rows = pl.ds(f * IN_DEV, IN_DEV)
                z_ref[0, rows, pl.ds(to, LANES)] = (a + b).astype(jnp.bfloat16)
                z_ref[1, rows, pl.ds(to, LANES)] = (a - b).astype(jnp.bfloat16)
            return carry

        lax.fori_loop(0, HALF // LANES, chunk, 0)

    g = jnp.concatenate([g_ref[0], g_ref[1]], 0)
    g_hi = g.astype(jnp.bfloat16)
    rest = g - g_hi.astype(jnp.float32)
    g_mid = rest.astype(jnp.bfloat16)
    g_low = (rest - g_mid.astype(jnp.float32)).astype(jnp.bfloat16)
    parts = jnp.concatenate([g_hi, g_mid, g_low], 0)
    picked = jnp.dot(parts, sel_ref[...], preferred_element_type=jnp.float32)
    picked = picked[0:32] + picked[32:64] + picked[64:96]
    real, imag = [], []
    for f in range(F_DEV):
        real.append([None, None])
        imag.append([None, None])
    for parity in range(2):
        spectra = jnp.dot(z_ref[parity], t_ref[0, parity], preferred_element_type=jnp.float32)
        g_re = picked[0:16, parity * LANES : (parity + 1) * LANES]
        g_im = picked[16:32, parity * LANES : (parity + 1) * LANES]
        for f in range(F_DEV):
            s_re = spectra[f * IN_DEV : (f + 1) * IN_DEV, :LANES]
            s_im = spectra[f * IN_DEV : (f + 1) * IN_DEV, LANES:]
            real[f][parity] = g_re * s_re - g_im * s_im
            imag[f][parity] = g_re * s_im + g_im * s_re
    for part, values in enumerate((real, imag)):
        arrays = swap_groups([values[j // 2][j % 2] for j in range(32)])
        for d in range(32):
            out_ref[pl.ds(d * IN_DEV, IN_DEV), pl.ds(part * LANES, LANES)] = arrays[d].astype(
                jnp.bfloat16
            )


def channelize(samples, prior, gains):
    return pl.pallas_call(
        channelize_kernel,
        grid=(BLOCKS,),
        in_specs=[
            pl.BlockSpec((IN_DEV, F_DEV * FRAME), lambda b: (0, 0)),
            pl.BlockSpec((IN_DEV, (TAPS - 1) * FRAME), lambda b: (0, 0)),
            pl.BlockSpec((TAPS, FRAME), lambda b: (0, 0)),
            pl.BlockSpec((1, 2, HALF, 2 * LANES), lambda b: (b, 0, 0, 0)),
            pl.BlockSpec((256, 256), lambda b: (0, 0)),
            pl.BlockSpec((2, IN_DEV, 256), lambda b: (0, 0, b)),
        ],
        out_specs=pl.BlockSpec((32 * IN_DEV, 256), lambda b: (b, 0)),
        out_shape=jax.ShapeDtypeStruct((INPUTS, 256), jnp.bfloat16),
        scratch_shapes=[pltpu.VMEM((2, F_DEV * IN_DEV, HALF), jnp.bfloat16)],
        compiler_params=pltpu.CompilerParams(vmem_limit_bytes=VMEM_LIMIT),
        cost_estimate=pl.CostEstimate(
            flops=2 * 256 * 1024 * 2048, bytes_accessed=7 * 1024 * 1024, transcendentals=0
        ),
        name="channelize",
    )(
        samples,
        prior,
        jnp.asarray(pfb_window()),
        jnp.asarray(folded_table()),
        jnp.asarray(gain_select()),
        gains,
    )


def beam_kernel(x_ref, pick_ref, order_ref, north_ref, fine_ref, out_ref, y_ref, beam_ref, power_ref):
    step = pl.program_id(0)
    cyl = lax.rem(step, CYL)
    fed = jnp.dot(pick_ref[...], x_ref[...], preferred_element_type=jnp.float32)
    both = jnp.dot(
        north_ref[...], fed.astype(jnp.bfloat16), preferred_element_type=jnp.float32
    )
    y_ref[cyl, 0] = both[:FEEDS, :LANES] + both[FEEDS:, LANES:]
    y_ref[cyl, 1] = both[:FEEDS, LANES:] - both[FEEDS:, :LANES]

    @pl.when(cyl == CYL - 1)
    def _():
        re = [y_ref[c, 0] for c in range(CYL)]
        im = [y_ref[c, 1] for c in range(CYL)]
        sum_re, dif_re = re[0] + re[2], re[0] - re[2]
        sum_im, dif_im = im[0] + im[2], im[0] - im[2]
        odd_re, odd_dif_re = re[1] + re[3], re[1] - re[3]
        odd_im, odd_dif_im = im[1] + im[3], im[1] - im[3]
        east = (
            (sum_re + odd_re, sum_im + odd_im),
            (dif_re + odd_dif_im, dif_im - odd_dif_re),
            (sum_re - odd_re, sum_im - odd_im),
            (dif_re - odd_dif_im, dif_im + odd_dif_re),
        )
        for e in range(CYL):
            beam_ref[pl.ds(e * FEEDS, FEEDS), :LANES] = east[e][0].astype(jnp.bfloat16)
            beam_ref[pl.ds(e * FEEDS, FEEDS), LANES:] = east[e][1].astype(jnp.bfloat16)
        fine = jnp.dot(beam_ref[...], fine_ref[...], preferred_element_type=jnp.float32)
        squares = fine * fine
        power = squares[:, :LANES] + squares[:, LANES:]

        @pl.when(step == CYL - 1)
        def _():
            power_ref[...] = power

        @pl.when(step == 2 * CYL - 1)
        def _():
            total = (0.25 * (power_ref[...] + power)).astype(jnp.bfloat16)
            out_ref[...] = jnp.dot(
                order_ref[...], total, preferred_element_type=jnp.float32
            ).astype(jnp.bfloat16)


def form_beams(piece, pick, order):
    return pl.pallas_call(
        beam_kernel,
        grid=(POLS * CYL,),
        in_specs=[
            pl.BlockSpec((INPUTS, 256), lambda s: (0, 0)),
            pl.BlockSpec((FEEDS, INPUTS), lambda s: (s, 0)),
            pl.BlockSpec((BEAMS, BEAMS), lambda s: (0, 0)),
            pl.BlockSpec((2 * FEEDS, FEEDS), lambda s: (0, 0)),
            pl.BlockSpec((256, 256), lambda s: (0, 0)),
        ],
        out_specs=pl.BlockSpec((BEAMS, LANES), lambda s: (0, 0)),
        out_shape=jax.ShapeDtypeStruct((BEAMS, LANES), jnp.bfloat16),
        scratch_shapes=[
            pltpu.VMEM((CYL, 2, FEEDS, LANES), jnp.float32),
            pltpu.VMEM((BEAMS, 256), jnp.bfloat16),
            pltpu.VMEM((BEAMS, LANES), jnp.float32),
        ],
        compiler_params=pltpu.CompilerParams(vmem_limit_bytes=VMEM_LIMIT),
        cost_estimate=pl.CostEstimate(
            flops=2 * 1024 * 1024 * 1500, bytes_accessed=12 * 1024 * 1024, transcendentals=0
        ),
        name="form_beams",
    )(piece, pick, order, jnp.asarray(north_table()), jnp.asarray(fine_table()))


def widen_kernel(x_ref, out_ref):
    for g in range(CHANNELS // CH_DEV):
        out_ref[0, :, g * LANES : (g + 1) * LANES] = x_ref[g].astype(jnp.float32)


def widen(power):
    slots = power.shape[0] * CH_DEV // CHANNELS
    return pl.pallas_call(
        widen_kernel,
        out_shape=jax.ShapeDtypeStruct((1, slots, CHANNELS * UPCH), jnp.float32),
        compiler_params=pltpu.CompilerParams(vmem_limit_bytes=VMEM_LIMIT),
        name="widen",
    )(power.reshape(CHANNELS // CH_DEV, slots, LANES))


def body(samples, gains, slot_inputs, beam_order):
    tail = samples[:, (F_DEV - TAPS + 1) * FRAME :]
    prior = from_behind(tail, "ta", 1)
    calibrated = channelize(samples, prior, gains)
    piece = lax.all_to_all(calibrated, "gx", split_axis=0, concat_axis=0, tiled=True)
    pick = (slot_inputs[:, None] == jnp.arange(INPUTS, dtype=jnp.int32)[None, :]).astype(jnp.bfloat16)
    order = (beam_order[:, None] == jnp.arange(BEAMS, dtype=jnp.int32)[None, :]).astype(jnp.bfloat16)
    power = form_beams(piece, pick, order)
    owned = lax.all_to_all(power, "gx", split_axis=0, concat_axis=0, tiled=True)
    return widen(owned)


def solution(mesh):
    placed = (P("gx", "ta"), P(None, "gx", None), P(), P())
    return jax.shard_map(
        body, mesh=mesh, in_specs=placed, out_specs=P("ta", "gx", None), check_vma=False
    )
```

```python
import math

import jax
import jax.numpy as jnp
import numpy as np
from jax import lax
from jax.experimental import pallas as pl
from jax.experimental.pallas import tpu as pltpu
from jax.sharding import PartitionSpec as P

CHANNELS = 1024
FRAME = 2 * CHANNELS
HALF = CHANNELS
FEEDS = 256
CYL = 4
POLS = 2
TAPS = 4
UPCH = 16
BEAMS = 1024
INPUTS = 2048
IN_DEV = 16
F_DEV = 16
CH_DEV = 8
BLOCKS = 4
LANES = 128
LATER = F_DEV - TAPS + 1
ALL_VMEM = 40 * 1024 * 1024
BEAM_VMEM = 32 * 1024 * 1024


def from_behind(block, axis, distance):
    devices = range(lax.axis_size(axis))
    route = [(i - distance, i) for i in devices if i - distance in devices]
    return lax.ppermute(block, axis, route)


def pfb_window():
    total = TAPS * FRAME
    places = np.arange(total, dtype=np.float64)
    centred = (places - (total - 1) * 0.5) / FRAME
    hann = 0.5 - 0.5 * np.cos(2.0 * math.pi * (places + 0.5) / total)
    window = np.sinc(centred) * hann
    window = window * np.sqrt(FRAME / np.sum(window * window))
    return window.reshape(TAPS, FRAME).astype(np.float32)


def folded_table():
    n = np.arange(HALF)
    lane = np.arange(LANES)
    out = np.zeros((BLOCKS, 2, HALF, 2 * LANES), np.float32)
    for block in range(BLOCKS):
        for parity in range(2):
            k = 256 * block + 8 * (lane // 4) + 2 * (lane % 4) + parity
            angle = 2.0 * math.pi / FRAME * (n[:, None] * k[None, :] % FRAME)
            out[block, parity, :, :LANES] = np.cos(angle) / math.sqrt(FRAME)
            out[block, parity, :, LANES:] = -np.sin(angle) / math.sqrt(FRAME)
    return out.astype(jnp.bfloat16)


def gain_select():
    lane = np.arange(LANES)
    out = np.zeros((256, 2 * LANES), np.float32)
    for parity in range(2):
        k = 8 * (lane // 4) + 2 * (lane % 4) + parity
        out[k, parity * LANES + lane] = 1.0
    return out.astype(jnp.bfloat16)


def north_table():
    index = np.arange(FEEDS)
    angle = 2.0 * math.pi / FEEDS * (index[:, None] * index[None, :] % FEEDS)
    scale = 1.0 / math.sqrt(FEEDS)
    table = np.concatenate([np.cos(angle), np.sin(angle)], 0) * scale
    return (table.astype(jnp.bfloat16).astype(np.float32) * 0.5).astype(jnp.bfloat16)


def fine_table():
    scale = 1.0 / math.sqrt(UPCH)
    out = np.zeros((2, F_DEV, 2, 4, 2, CH_DEV, UPCH), np.float32)
    j = np.arange(UPCH)
    angle = 2.0 * math.pi / UPCH * (j[:, None] * j[None, :] % UPCH)
    cosine, sine = np.cos(angle) * scale, np.sin(angle) * scale
    for parity in range(2):
        for h in range(4):
            channel = 2 * h + parity
            out[0, :, parity, h, 0, channel, :] = cosine
            out[0, :, parity, h, 1, channel, :] = -sine
            out[1, :, parity, h, 0, channel, :] = sine
            out[1, :, parity, h, 1, channel, :] = cosine
    return out.reshape(256, 256).astype(jnp.bfloat16)


def swap_groups(arrays):
    lane = lax.broadcasted_iota(jnp.int32, arrays[0].shape, 1) // 4
    arrays = list(arrays)
    for bit in (16, 8, 4, 2, 1):
        low = (lane & bit) == 0
        for j in range(32):
            if j & bit:
                continue
            a, b = arrays[j], arrays[j | bit]
            arrays[j] = jnp.where(low, a, pltpu.roll(b, 4 * bit, 1))
            arrays[j | bit] = jnp.where(low, pltpu.roll(a, LANES - 4 * bit, 1), b)
    return arrays


def filter_frames(frames, w, first, count):
    rows = []
    for f in range(first, first + count):
        total = frames[f - TAPS + 1] * w[0]
        for t in range(1, TAPS):
            total = total + frames[f - TAPS + 1 + t] * w[t]
        rows.append(total)
    return rows


def fold_frames(parts, w_ref, z_ref, count):
    def chunk(c, carry):
        halves = []
        for half in range(2):
            at = pl.multiple_of(half * HALF + c * LANES, LANES)
            w = [w_ref[t : t + 1, pl.ds(at, LANES)] for t in range(TAPS)]
            frames = []
            for ref in parts:
                for f in range(ref.shape[1] // FRAME):
                    frames.append(ref[:, pl.ds(f * FRAME + at, LANES)].astype(jnp.float32))
            halves.append(filter_frames(frames, w, TAPS - 1, count))
        to = pl.ds(pl.multiple_of(c * LANES, LANES), LANES)
        for f in range(count):
            a, b = halves[0][f], halves[1][f]
            z_ref[0, pl.ds(f * IN_DEV, IN_DEV), to] = (a + b).astype(jnp.bfloat16)
            z_ref[1, pl.ds(f * IN_DEV, IN_DEV), to] = (a - b).astype(jnp.bfloat16)
        return carry

    lax.fori_loop(0, HALF // LANES, chunk, 0)


def calibrate(z, table, gain_re, gain_im):
    spectra = jnp.dot(z, table, preferred_element_type=jnp.float32)
    real, imag = [], []
    for f in range(z.shape[0] // IN_DEV):
        s_re = spectra[f * IN_DEV : (f + 1) * IN_DEV, :LANES]
        s_im = spectra[f * IN_DEV : (f + 1) * IN_DEV, LANES:]
        real.append(gain_re * s_re - gain_im * s_im)
        imag.append(gain_re * s_im + gain_im * s_re)
    return real, imag


def later_kernel(
    x_hbm, w_hbm, t_hbm, sel_hbm, g_hbm, x_ref, w_ref, t_ref, out_ref, picked_ref, sel_ref, g_ref, z_ref, sems
):
    copies = [
        pltpu.make_async_copy(x_hbm, x_ref, sems.at[0]),
        pltpu.make_async_copy(w_hbm, w_ref, sems.at[1]),
        pltpu.make_async_copy(sel_hbm, sel_ref, sems.at[2]),
        pltpu.make_async_copy(g_hbm, g_ref, sems.at[3]),
    ]
    for block in range(BLOCKS):
        copies.append(pltpu.make_async_copy(t_hbm.at[block], t_ref.at[block], sems.at[4 + block]))
    for copy in copies:
        copy.start()
    for copy in copies[:2]:
        copy.wait()
    fold_frames([x_ref], w_ref, z_ref, LATER)
    for copy in copies[2:4]:
        copy.wait()
    for block in range(BLOCKS):
        columns = slice(block * 256, (block + 1) * 256)
        g = jnp.concatenate([g_ref[0, :, columns], g_ref[1, :, columns]], 0)
        g_hi = g.astype(jnp.bfloat16)
        rest = g - g_hi.astype(jnp.float32)
        g_mid = rest.astype(jnp.bfloat16)
        g_low = (rest - g_mid.astype(jnp.float32)).astype(jnp.bfloat16)
        parts = jnp.concatenate([g_hi, g_mid, g_low], 0)
        picked = jnp.dot(parts, sel_ref[...], preferred_element_type=jnp.float32)
        picked_ref[block] = picked[0:32] + picked[32:64] + picked[64:96]
    for block in range(BLOCKS):
        copies[4 + block].wait()
        picked = picked_ref[block]
        for parity in range(2):
            lanes = slice(parity * LANES, (parity + 1) * LANES)
            real, imag = calibrate(
                z_ref[parity], t_ref[block, parity], picked[0:16, lanes], picked[16:32, lanes]
            )
            for f in range(LATER):
                rows = pl.ds(f * IN_DEV, IN_DEV)
                out_ref[block, 0, parity, rows, :] = real[f].astype(jnp.bfloat16)
                out_ref[block, 1, parity, rows, :] = imag[f].astype(jnp.bfloat16)


def first_kernel(x_ref, prior_ref, w_ref, t_ref, picked_ref, later_ref, out_hbm, z_ref, out_ref, sems):
    fold_frames([prior_ref, x_ref.at[:, : (TAPS - 1) * FRAME]], w_ref, z_ref, TAPS - 1)
    copies = []
    for block in range(BLOCKS):
        picked = picked_ref[block]
        values = [[None] * 32, [None] * 32]
        for parity in range(2):
            lanes = slice(parity * LANES, (parity + 1) * LANES)
            early = calibrate(
                z_ref[parity], t_ref[block, parity], picked[0:16, lanes], picked[16:32, lanes]
            )
            for part in range(2):
                for f in range(TAPS - 1):
                    values[part][2 * f + parity] = early[part][f].astype(jnp.bfloat16)
                for f in range(LATER):
                    rows = pl.ds(f * IN_DEV, IN_DEV)
                    values[part][2 * (f + TAPS - 1) + parity] = later_ref[block, part, parity, rows, :]
        for part in range(2):
            arrays = swap_groups(values[part])
            for d in range(32):
                rows = pl.ds((block * 32 + d) * IN_DEV, IN_DEV)
                out_ref[rows, pl.ds(part * LANES, LANES)] = arrays[d]
        rows = pl.ds(block * 32 * IN_DEV, 32 * IN_DEV)
        copies.append(pltpu.make_async_copy(out_ref.at[rows], out_hbm.at[rows], sems.at[block]))
        copies[block].start()
    for copy in copies:
        copy.wait()


IN_VMEM = pl.BlockSpec(memory_space=pltpu.VMEM)
IN_HBM = pl.BlockSpec(memory_space=pltpu.HBM)


def channelize_later(samples, gains):
    table = folded_table()
    return pl.pallas_call(
        later_kernel,
        in_specs=[IN_HBM] * 5,
        out_specs=[IN_VMEM] * 5,
        out_shape=[
            pltpu.VMEM((IN_DEV, F_DEV * FRAME), jnp.bfloat16),
            pltpu.VMEM((TAPS, FRAME), jnp.float32),
            pltpu.VMEM(table.shape, jnp.bfloat16),
            pltpu.VMEM((BLOCKS, 2, 2, LATER * IN_DEV, LANES), jnp.bfloat16),
            pltpu.VMEM((BLOCKS, 2 * IN_DEV, 2 * LANES), jnp.float32),
        ],
        scratch_shapes=[
            pltpu.VMEM((256, 256), jnp.bfloat16),
            pltpu.VMEM((2, IN_DEV, CHANNELS), jnp.float32),
            pltpu.VMEM((2, LATER * IN_DEV, HALF), jnp.bfloat16),
            pltpu.SemaphoreType.DMA((4 + BLOCKS,)),
        ],
        compiler_params=pltpu.CompilerParams(vmem_limit_bytes=ALL_VMEM),
        cost_estimate=pl.CostEstimate(
            flops=2 * 256 * 1024 * 2048, bytes_accessed=7 * 1024 * 1024, transcendentals=0
        ),
        name="channelize_later",
    )(
        *(
            pltpu.with_memory_space_constraint(x, pltpu.HBM)
            for x in (
                samples,
                jnp.asarray(pfb_window()),
                jnp.asarray(table),
                jnp.asarray(gain_select()),
                gains,
            )
        )
    )


def channelize_first(samples, prior, window, table, picked, later):
    return pl.pallas_call(
        first_kernel,
        in_specs=[IN_VMEM] * 6,
        out_specs=IN_HBM,
        out_shape=jax.ShapeDtypeStruct((INPUTS, 256), jnp.bfloat16),
        scratch_shapes=[
            pltpu.VMEM((2, (TAPS - 1) * IN_DEV, HALF), jnp.bfloat16),
            pltpu.VMEM((INPUTS, 256), jnp.bfloat16),
            pltpu.SemaphoreType.DMA((BLOCKS,)),
        ],
        compiler_params=pltpu.CompilerParams(vmem_limit_bytes=BEAM_VMEM),
        cost_estimate=pl.CostEstimate(
            flops=2 * 48 * 1024 * 2048, bytes_accessed=7 * 1024 * 1024, transcendentals=0
        ),
        name="channelize_first",
    )(samples, prior, window, table, picked, later)


def beam_kernel(x_ref, pick_ref, order_ref, north_ref, fine_ref, out_ref, fed_ref, beam_ref, power_ref):
    for pol in range(POLS):
        for cyl in range(CYL):
            rows = pl.ds((pol * CYL + cyl) * FEEDS, FEEDS)
            fed_ref[rows, :] = jnp.dot(
                pick_ref[rows, :], x_ref[...], preferred_element_type=jnp.float32
            ).astype(jnp.bfloat16)
        re, im = [], []
        for cyl in range(CYL):
            rows = pl.ds((pol * CYL + cyl) * FEEDS, FEEDS)
            both = jnp.dot(north_ref[...], fed_ref[rows, :], preferred_element_type=jnp.float32)
            re.append(both[:FEEDS, :LANES] + both[FEEDS:, LANES:])
            im.append(both[:FEEDS, LANES:] - both[FEEDS:, :LANES])
        sum_re, dif_re = re[0] + re[2], re[0] - re[2]
        sum_im, dif_im = im[0] + im[2], im[0] - im[2]
        odd_re, odd_dif_re = re[1] + re[3], re[1] - re[3]
        odd_im, odd_dif_im = im[1] + im[3], im[1] - im[3]
        east = (
            (sum_re + odd_re, sum_im + odd_im),
            (dif_re + odd_dif_im, dif_im - odd_dif_re),
            (sum_re - odd_re, sum_im - odd_im),
            (dif_re - odd_dif_im, dif_im + odd_dif_re),
        )
        for e in range(CYL):
            beam_ref[pl.ds(e * FEEDS, FEEDS), :LANES] = east[e][0].astype(jnp.bfloat16)
            beam_ref[pl.ds(e * FEEDS, FEEDS), LANES:] = east[e][1].astype(jnp.bfloat16)
        fine = jnp.dot(beam_ref[...], fine_ref[...], preferred_element_type=jnp.float32)
        squares = fine * fine
        power = squares[:, :LANES] + squares[:, LANES:]
        if pol == 0:
            power_ref[...] = power
        else:
            total = (0.25 * (power_ref[...] + power)).astype(jnp.bfloat16)
            out_ref[...] = jnp.dot(
                order_ref[...], total, preferred_element_type=jnp.float32
            ).astype(jnp.bfloat16)


def form_beams(piece, pick, order):
    return pl.pallas_call(
        beam_kernel,
        in_specs=[pl.BlockSpec(memory_space=pltpu.VMEM)] * 5,
        out_specs=pl.BlockSpec(memory_space=pltpu.VMEM),
        out_shape=jax.ShapeDtypeStruct((BEAMS, LANES), jnp.bfloat16),
        scratch_shapes=[
            pltpu.VMEM((INPUTS, 256), jnp.bfloat16),
            pltpu.VMEM((BEAMS, 256), jnp.bfloat16),
            pltpu.VMEM((BEAMS, LANES), jnp.float32),
        ],
        compiler_params=pltpu.CompilerParams(vmem_limit_bytes=BEAM_VMEM),
        cost_estimate=pl.CostEstimate(
            flops=2 * 1024 * 1024 * 1500, bytes_accessed=12 * 1024 * 1024, transcendentals=0
        ),
        name="form_beams",
    )(piece, pick, order, jnp.asarray(north_table()), jnp.asarray(fine_table()))


def widen_kernel(x_ref, out_ref):
    for g in range(CHANNELS // CH_DEV):
        out_ref[0, :, g * LANES : (g + 1) * LANES] = x_ref[g].astype(jnp.float32)


def widen(power):
    slots = power.shape[0] * CH_DEV // CHANNELS
    return pl.pallas_call(
        widen_kernel,
        out_shape=jax.ShapeDtypeStruct((1, slots, CHANNELS * UPCH), jnp.float32),
        compiler_params=pltpu.CompilerParams(vmem_limit_bytes=BEAM_VMEM),
        name="widen",
    )(power.reshape(CHANNELS // CH_DEV, slots, LANES))


def body(samples, gains, slot_inputs, beam_order):
    tail = samples[:, (F_DEV - TAPS + 1) * FRAME :]
    prior = from_behind(tail, "ta", 1)
    held, window, table, later, picked = channelize_later(samples, gains)
    calibrated = channelize_first(held, prior, window, table, picked, later)
    piece = lax.all_to_all(calibrated, "gx", split_axis=0, concat_axis=0, tiled=True)
    pick = (slot_inputs[:, None] == jnp.arange(INPUTS, dtype=jnp.int32)[None, :]).astype(jnp.bfloat16)
    order = (beam_order[:, None] == jnp.arange(BEAMS, dtype=jnp.int32)[None, :]).astype(jnp.bfloat16)
    power = form_beams(piece, pick, order)
    owned = lax.all_to_all(power, "gx", split_axis=0, concat_axis=0, tiled=True)
    return widen(owned)


def solution(mesh):
    placed = (P("gx", "ta"), P(None, "gx", None), P(), P())
    return jax.shard_map(
        body, mesh=mesh, in_specs=placed, out_specs=P("ta", "gx", None), check_vma=False
    )
```

```python
import math

import jax
import jax.numpy as jnp
import numpy as np
from jax import lax
from jax.experimental import pallas as pl
from jax.experimental.pallas import tpu as pltpu
from jax.sharding import PartitionSpec as P

CHANNELS = 1024
FRAME = 2 * CHANNELS
HALF = CHANNELS
FEEDS = 256
CYL = 4
POLS = 2
TAPS = 4
UPCH = 16
BEAMS = 1024
INPUTS = 2048
IN_DEV = 16
F_DEV = 16
CH_DEV = 8
BLOCKS = 4
LANES = 128
LATER = F_DEV - TAPS + 1
ALL_VMEM = 40 * 1024 * 1024
BEAM_VMEM = 32 * 1024 * 1024
HEAD = 256
MADE = 1024
RING = np.random.RandomState(3).permutation(128).tolist()


def from_behind(block, axis, distance):
    devices = range(lax.axis_size(axis))
    route = [(i - distance, i) for i in devices if i - distance in devices]
    return lax.ppermute(block, axis, route)


def exchange(block):
    return lax.all_to_all(
        block, "gx", split_axis=0, concat_axis=0, axis_index_groups=[RING], tiled=True
    )


def pfb_window():
    total = TAPS * FRAME
    places = np.arange(total, dtype=np.float64)
    centred = (places - (total - 1) * 0.5) / FRAME
    hann = 0.5 - 0.5 * np.cos(2.0 * math.pi * (places + 0.5) / total)
    window = np.sinc(centred) * hann
    window = window * np.sqrt(FRAME / np.sum(window * window))
    return window.reshape(TAPS, FRAME).astype(np.float32)


def folded_table():
    n = np.arange(HALF)
    lane = np.arange(LANES)
    out = np.zeros((BLOCKS, 2, HALF, 2 * LANES), np.float32)
    for block in range(BLOCKS):
        for parity in range(2):
            k = 256 * block + 8 * (lane // 4) + 2 * (lane % 4) + parity
            angle = 2.0 * math.pi / FRAME * (n[:, None] * k[None, :] % FRAME)
            out[block, parity, :, :LANES] = np.cos(angle) / math.sqrt(FRAME)
            out[block, parity, :, LANES:] = -np.sin(angle) / math.sqrt(FRAME)
    return out.astype(jnp.bfloat16)


def gain_select():
    lane = np.arange(LANES)
    out = np.zeros((256, 2 * LANES), np.float32)
    for parity in range(2):
        k = 8 * (lane // 4) + 2 * (lane % 4) + parity
        out[k, parity * LANES + lane] = 1.0
    return out.astype(jnp.bfloat16)


def north_table():
    index = np.arange(FEEDS)
    angle = 2.0 * math.pi / FEEDS * (index[:, None] * index[None, :] % FEEDS)
    scale = 1.0 / math.sqrt(FEEDS)
    table = np.concatenate([np.cos(angle), np.sin(angle)], 0) * scale
    return (table.astype(jnp.bfloat16).astype(np.float32) * 0.5).astype(jnp.bfloat16)


def fine_table():
    scale = 1.0 / math.sqrt(UPCH)
    out = np.zeros((2, F_DEV, 2, 4, 2, CH_DEV, UPCH), np.float32)
    j = np.arange(UPCH)
    angle = 2.0 * math.pi / UPCH * (j[:, None] * j[None, :] % UPCH)
    cosine, sine = np.cos(angle) * scale, np.sin(angle) * scale
    for parity in range(2):
        for h in range(4):
            channel = 2 * h + parity
            out[0, :, parity, h, 0, channel, :] = cosine
            out[0, :, parity, h, 1, channel, :] = -sine
            out[1, :, parity, h, 0, channel, :] = sine
            out[1, :, parity, h, 1, channel, :] = cosine
    return out.reshape(256, 256).astype(jnp.bfloat16)


def swap_groups(arrays):
    lane = lax.broadcasted_iota(jnp.int32, arrays[0].shape, 1) // 4
    arrays = list(arrays)
    for bit in (16, 8, 4, 2, 1):
        low = (lane & bit) == 0
        for j in range(32):
            if j & bit:
                continue
            a, b = arrays[j], arrays[j | bit]
            arrays[j] = jnp.where(low, a, pltpu.roll(b, 4 * bit, 1))
            arrays[j | bit] = jnp.where(low, pltpu.roll(a, LANES - 4 * bit, 1), b)
    return arrays


def filter_frames(frames, w, first, count):
    rows = []
    for f in range(first, first + count):
        total = frames[f - TAPS + 1] * w[0]
        for t in range(1, TAPS):
            total = total + frames[f - TAPS + 1 + t] * w[t]
        rows.append(total)
    return rows


def fold_frames(parts, w_ref, z_ref, count):
    def chunk(c, carry):
        halves = []
        for half in range(2):
            at = pl.multiple_of(half * HALF + c * LANES, LANES)
            w = [w_ref[t : t + 1, pl.ds(at, LANES)] for t in range(TAPS)]
            frames = []
            for ref in parts:
                for f in range(ref.shape[1] // FRAME):
                    frames.append(ref[:, pl.ds(f * FRAME + at, LANES)].astype(jnp.float32))
            halves.append(filter_frames(frames, w, TAPS - 1, count))
        to = pl.ds(pl.multiple_of(c * LANES, LANES), LANES)
        for f in range(count):
            a, b = halves[0][f], halves[1][f]
            z_ref[0, pl.ds(f * IN_DEV, IN_DEV), to] = (a + b).astype(jnp.bfloat16)
            z_ref[1, pl.ds(f * IN_DEV, IN_DEV), to] = (a - b).astype(jnp.bfloat16)
        return carry

    lax.fori_loop(0, HALF // LANES, chunk, 0)


def calibrate(z, table, gain_re, gain_im):
    spectra = jnp.dot(z, table, preferred_element_type=jnp.float32)
    real, imag = [], []
    for f in range(z.shape[0] // IN_DEV):
        s_re = spectra[f * IN_DEV : (f + 1) * IN_DEV, :LANES]
        s_im = spectra[f * IN_DEV : (f + 1) * IN_DEV, LANES:]
        real.append(gain_re * s_re - gain_im * s_im)
        imag.append(gain_re * s_im + gain_im * s_re)
    return real, imag


def later_kernel(
    x_hbm, w_hbm, t_hbm, sel_hbm, g_hbm, x_ref, w_ref, t_ref, out_ref, picked_ref, sel_ref, g_ref, z_ref, sems
):
    copies = [
        pltpu.make_async_copy(x_hbm, x_ref, sems.at[0]),
        pltpu.make_async_copy(w_hbm, w_ref, sems.at[1]),
        pltpu.make_async_copy(sel_hbm, sel_ref, sems.at[2]),
        pltpu.make_async_copy(g_hbm, g_ref, sems.at[3]),
    ]
    for block in range(BLOCKS):
        copies.append(pltpu.make_async_copy(t_hbm.at[block], t_ref.at[block], sems.at[4 + block]))
    for copy in copies:
        copy.start()
    for copy in copies[:2]:
        copy.wait()
    fold_frames([x_ref], w_ref, z_ref, LATER)
    for copy in copies[2:4]:
        copy.wait()
    for block in range(BLOCKS):
        columns = slice(block * 256, (block + 1) * 256)
        g = jnp.concatenate([g_ref[0, :, columns], g_ref[1, :, columns]], 0)
        g_hi = g.astype(jnp.bfloat16)
        rest = g - g_hi.astype(jnp.float32)
        g_mid = rest.astype(jnp.bfloat16)
        g_low = (rest - g_mid.astype(jnp.float32)).astype(jnp.bfloat16)
        parts = jnp.concatenate([g_hi, g_mid, g_low], 0)
        picked = jnp.dot(parts, sel_ref[...], preferred_element_type=jnp.float32)
        picked_ref[block] = picked[0:32] + picked[32:64] + picked[64:96]
    for block in range(BLOCKS):
        copies[4 + block].wait()
        picked = picked_ref[block]
        for parity in range(2):
            lanes = slice(parity * LANES, (parity + 1) * LANES)
            real, imag = calibrate(
                z_ref[parity], t_ref[block, parity], picked[0:16, lanes], picked[16:32, lanes]
            )
            for f in range(LATER):
                rows = pl.ds(f * IN_DEV, IN_DEV)
                out_ref[block, 0, parity, rows, :] = real[f].astype(jnp.bfloat16)
                out_ref[block, 1, parity, rows, :] = imag[f].astype(jnp.bfloat16)


def first_kernel(x_ref, prior_ref, w_ref, t_ref, picked_ref, later_ref, out_hbm, z_ref, out_ref, sems):
    fold_frames([prior_ref, x_ref.at[:, : (TAPS - 1) * FRAME]], w_ref, z_ref, TAPS - 1)
    copies = []
    for block in range(BLOCKS):
        picked = picked_ref[block]
        values = [[None] * 32, [None] * 32]
        for parity in range(2):
            lanes = slice(parity * LANES, (parity + 1) * LANES)
            early = calibrate(
                z_ref[parity], t_ref[block, parity], picked[0:16, lanes], picked[16:32, lanes]
            )
            for part in range(2):
                for f in range(TAPS - 1):
                    values[part][2 * f + parity] = early[part][f].astype(jnp.bfloat16)
                for f in range(LATER):
                    rows = pl.ds(f * IN_DEV, IN_DEV)
                    values[part][2 * (f + TAPS - 1) + parity] = later_ref[block, part, parity, rows, :]
        for part in range(2):
            arrays = swap_groups(values[part])
            for d in range(32):
                rows = pl.ds((block * 32 + d) * IN_DEV, IN_DEV)
                out_ref[rows, pl.ds(part * LANES, LANES)] = arrays[d]
        rows = pl.ds(block * 32 * IN_DEV, 32 * IN_DEV)
        copies.append(pltpu.make_async_copy(out_ref.at[rows], out_hbm.at[rows], sems.at[block]))
        copies[block].start()
    for copy in copies:
        copy.wait()


IN_VMEM = pl.BlockSpec(memory_space=pltpu.VMEM)
IN_HBM = pl.BlockSpec(memory_space=pltpu.HBM)


def channelize_later(samples, gains):
    table = folded_table()
    return pl.pallas_call(
        later_kernel,
        in_specs=[IN_HBM] * 5,
        out_specs=[IN_VMEM] * 5,
        out_shape=[
            pltpu.VMEM((IN_DEV, F_DEV * FRAME), jnp.bfloat16),
            pltpu.VMEM((TAPS, FRAME), jnp.float32),
            pltpu.VMEM(table.shape, jnp.bfloat16),
            pltpu.VMEM((BLOCKS, 2, 2, LATER * IN_DEV, LANES), jnp.bfloat16),
            pltpu.VMEM((BLOCKS, 2 * IN_DEV, 2 * LANES), jnp.float32),
        ],
        scratch_shapes=[
            pltpu.VMEM((256, 256), jnp.bfloat16),
            pltpu.VMEM((2, IN_DEV, CHANNELS), jnp.float32),
            pltpu.VMEM((2, LATER * IN_DEV, HALF), jnp.bfloat16),
            pltpu.SemaphoreType.DMA((4 + BLOCKS,)),
        ],
        compiler_params=pltpu.CompilerParams(vmem_limit_bytes=ALL_VMEM),
        cost_estimate=pl.CostEstimate(
            flops=2 * 256 * 1024 * 2048, bytes_accessed=7 * 1024 * 1024, transcendentals=0
        ),
        name="channelize_later",
    )(
        *(
            pltpu.with_memory_space_constraint(x, pltpu.HBM)
            for x in (
                samples,
                jnp.asarray(pfb_window()),
                jnp.asarray(table),
                jnp.asarray(gain_select()),
                gains,
            )
        )
    )


def channelize_first(samples, prior, window, table, picked, later):
    return pl.pallas_call(
        first_kernel,
        in_specs=[IN_VMEM] * 6,
        out_specs=IN_HBM,
        out_shape=jax.ShapeDtypeStruct((INPUTS, 256), jnp.bfloat16),
        scratch_shapes=[
            pltpu.VMEM((2, (TAPS - 1) * IN_DEV, HALF), jnp.bfloat16),
            pltpu.VMEM((INPUTS, 256), jnp.bfloat16),
            pltpu.SemaphoreType.DMA((BLOCKS,)),
        ],
        compiler_params=pltpu.CompilerParams(vmem_limit_bytes=BEAM_VMEM),
        cost_estimate=pl.CostEstimate(
            flops=2 * 48 * 1024 * 2048, bytes_accessed=7 * 1024 * 1024, transcendentals=0
        ),
        name="channelize_first",
    )(samples, prior, window, table, picked, later)


def one_hot_kernel(slots_ref, order_ref, ids_ref, head_ref, rest_hbm, turn_hbm, rest_ref, turn_ref, sems):
    slots = jnp.transpose(slots_ref[...])
    copies = []
    for block in [*range(HEAD // LANES), *range(MADE // LANES, INPUTS // LANES)]:
        hot = jnp.where(slots[:, block : block + 1] == ids_ref[...], 1.0, 0.0).astype(jnp.bfloat16)
        at = block * LANES
        if at < HEAD:
            head_ref[pl.ds(at, LANES), :] = hot
            continue
        rows = pl.ds(at - MADE, LANES)
        rest_ref[rows, :] = hot
        copies.append(
            pltpu.make_async_copy(rest_ref.at[rows], rest_hbm.at[rows], sems.at[len(copies)])
        )
        copies[-1].start()
    beams = jnp.transpose(order_ref[...])
    index = lax.broadcasted_iota(jnp.int32, (2 * CH_DEV, BEAMS), 1)
    for pair in range(BEAMS // (2 * CH_DEV)):
        columns = []
        for g in RING[2 * pair : 2 * pair + 2]:
            row = g * CH_DEV % LANES
            at = g * CH_DEV // LANES
            columns.append(beams[row : row + CH_DEV, at : at + 1])
        turn_ref[pl.ds(pair * 2 * CH_DEV, 2 * CH_DEV), :] = jnp.where(
            jnp.concatenate(columns, 0) == index, 1.0, 0.0
        ).astype(jnp.bfloat16)
    copies.append(pltpu.make_async_copy(turn_ref, turn_hbm, sems.at[len(copies)]))
    copies[-1].start()
    for copy in copies:
        copy.wait()


def one_hots(slots, beam_order, ids):
    return pl.pallas_call(
        one_hot_kernel,
        in_specs=[IN_VMEM] * 3,
        out_specs=[IN_VMEM, IN_HBM, IN_HBM],
        out_shape=[
            pltpu.VMEM((HEAD, INPUTS), jnp.bfloat16),
            pltpu.HBM((INPUTS - MADE, INPUTS), jnp.bfloat16),
            pltpu.HBM((BEAMS, BEAMS), jnp.bfloat16),
        ],
        scratch_shapes=[
            pltpu.VMEM((INPUTS - MADE, INPUTS), jnp.bfloat16),
            pltpu.VMEM((BEAMS, BEAMS), jnp.bfloat16),
            pltpu.SemaphoreType.DMA(((INPUTS - MADE) // LANES + 1,)),
        ],
        compiler_params=pltpu.CompilerParams(vmem_limit_bytes=BEAM_VMEM),
        cost_estimate=pl.CostEstimate(
            flops=20 * 1024 * 1024, bytes_accessed=10 * 1024 * 1024, transcendentals=0
        ),
        name="one_hots",
    )(
        slots,
        beam_order.reshape(BEAMS // LANES, LANES),
        ids,
    )


def beam_kernel(
    x_ref,
    head_ref,
    rest_hbm,
    turn_hbm,
    north_ref,
    fine_ref,
    slots_ref,
    ids_ref,
    out_ref,
    made_ref,
    rest_ref,
    turn_ref,
    fed_ref,
    beam_ref,
    power_ref,
    sems,
):
    rest_copy = pltpu.make_async_copy(rest_hbm, rest_ref, sems.at[0])
    turn_copy = pltpu.make_async_copy(turn_hbm, turn_ref, sems.at[1])
    rest_copy.start()
    turn_copy.start()
    slots = jnp.transpose(slots_ref[...])
    for pol in range(POLS):
        for cyl in range(CYL):
            at = (pol * CYL + cyl) * FEEDS
            if at < HEAD:
                pick = head_ref[pl.ds(at, FEEDS), :]
            elif at < MADE:
                for block in range(at // LANES, (at + FEEDS) // LANES):
                    made_ref[pl.ds(block * LANES - HEAD, LANES), :] = jnp.where(
                        slots[:, block : block + 1] == ids_ref[...], 1.0, 0.0
                    ).astype(jnp.bfloat16)
                pick = made_ref[pl.ds(at - HEAD, FEEDS), :]
            else:
                if at == MADE:
                    rest_copy.wait()
                pick = rest_ref[pl.ds(at - MADE, FEEDS), :]
            fed_ref[pl.ds(at, FEEDS), :] = jnp.dot(
                pick, x_ref[...], preferred_element_type=jnp.float32
            ).astype(jnp.bfloat16)
        re, im = [], []
        for cyl in range(CYL):
            rows = pl.ds((pol * CYL + cyl) * FEEDS, FEEDS)
            both = jnp.dot(north_ref[...], fed_ref[rows, :], preferred_element_type=jnp.float32)
            re.append(both[:FEEDS, :LANES] + both[FEEDS:, LANES:])
            im.append(both[:FEEDS, LANES:] - both[FEEDS:, :LANES])
        sum_re, dif_re = re[0] + re[2], re[0] - re[2]
        sum_im, dif_im = im[0] + im[2], im[0] - im[2]
        odd_re, odd_dif_re = re[1] + re[3], re[1] - re[3]
        odd_im, odd_dif_im = im[1] + im[3], im[1] - im[3]
        east = (
            (sum_re + odd_re, sum_im + odd_im),
            (dif_re + odd_dif_im, dif_im - odd_dif_re),
            (sum_re - odd_re, sum_im - odd_im),
            (dif_re - odd_dif_im, dif_im + odd_dif_re),
        )
        for e in range(CYL):
            beam_ref[pl.ds(e * FEEDS, FEEDS), :LANES] = east[e][0].astype(jnp.bfloat16)
            beam_ref[pl.ds(e * FEEDS, FEEDS), LANES:] = east[e][1].astype(jnp.bfloat16)
        fine = jnp.dot(beam_ref[...], fine_ref[...], preferred_element_type=jnp.float32)
        squares = fine * fine
        power = squares[:, :LANES] + squares[:, LANES:]
        if pol == 0:
            power_ref[...] = power
        else:
            total = (0.25 * (power_ref[...] + power)).astype(jnp.bfloat16)
            turn_copy.wait()
            out_ref[...] = jnp.dot(
                turn_ref[...], total, preferred_element_type=jnp.float32
            ).astype(jnp.bfloat16)


def form_beams(piece, head, rest, turn, slots, ids):
    return pl.pallas_call(
        beam_kernel,
        in_specs=[IN_VMEM, IN_VMEM, IN_HBM, IN_HBM, IN_VMEM, IN_VMEM, IN_VMEM, IN_VMEM],
        out_specs=IN_VMEM,
        out_shape=jax.ShapeDtypeStruct((BEAMS, LANES), jnp.bfloat16),
        scratch_shapes=[
            pltpu.VMEM((MADE - HEAD, INPUTS), jnp.bfloat16),
            pltpu.VMEM((INPUTS - MADE, INPUTS), jnp.bfloat16),
            pltpu.VMEM((BEAMS, BEAMS), jnp.bfloat16),
            pltpu.VMEM((INPUTS, 256), jnp.bfloat16),
            pltpu.VMEM((BEAMS, 256), jnp.bfloat16),
            pltpu.VMEM((BEAMS, LANES), jnp.float32),
            pltpu.SemaphoreType.DMA((2,)),
        ],
        compiler_params=pltpu.CompilerParams(vmem_limit_bytes=BEAM_VMEM),
        cost_estimate=pl.CostEstimate(
            flops=2 * 1024 * 1024 * 1500, bytes_accessed=12 * 1024 * 1024, transcendentals=0
        ),
        name="form_beams",
    )(
        piece,
        head,
        pltpu.with_memory_space_constraint(rest, pltpu.HBM),
        pltpu.with_memory_space_constraint(turn, pltpu.HBM),
        jnp.asarray(north_table()),
        jnp.asarray(fine_table()),
        slots,
        ids,
    )


def widen_kernel(x_ref, out_ref):
    for g in range(CHANNELS // CH_DEV):
        out_ref[0, :, g * LANES : (g + 1) * LANES] = x_ref[g].astype(jnp.float32)


def widen(power):
    slots = power.shape[0] * CH_DEV // CHANNELS
    return pl.pallas_call(
        widen_kernel,
        out_shape=jax.ShapeDtypeStruct((1, slots, CHANNELS * UPCH), jnp.float32),
        compiler_params=pltpu.CompilerParams(vmem_limit_bytes=BEAM_VMEM),
        name="widen",
    )(power.reshape(CHANNELS // CH_DEV, slots, LANES))


def body(samples, gains, slot_inputs, beam_order):
    tail = samples[:, (F_DEV - TAPS + 1) * FRAME :]
    prior = from_behind(tail, "ta", 1)
    held, window, table, later, picked = channelize_later(samples, gains)
    calibrated = channelize_first(held, prior, window, table, picked, later)
    piece = exchange(calibrated)
    ids = np.concatenate([np.arange(g * IN_DEV, (g + 1) * IN_DEV) for g in RING])
    ids = jnp.asarray(ids[None, :], jnp.int32)
    slots = slot_inputs.reshape(INPUTS // LANES, LANES)
    head, rest, turn = one_hots(slots, beam_order, ids)
    power = form_beams(piece, head, rest, turn, slots, ids)
    owned = exchange(power)
    return widen(owned)


def solution(mesh):
    placed = (P("gx", "ta"), P(None, "gx", None), P(), P())
    return jax.shard_map(
        body, mesh=mesh, in_specs=placed, out_specs=P("ta", "gx", None), check_vma=False
    )
```

```python
import math

import jax
import jax.numpy as jnp
import numpy as np
from jax import lax
from jax.experimental import pallas as pl
from jax.experimental.pallas import tpu as pltpu
from jax.sharding import PartitionSpec as P

CHANNELS = 1024
FRAME = 2 * CHANNELS
HALF = CHANNELS
FEEDS = 256
CYL = 4
POLS = 2
TAPS = 4
UPCH = 16
BEAMS = 1024
INPUTS = 2048
IN_DEV = 16
F_DEV = 16
CH_DEV = 8
BLOCKS = 4
LANES = 128
LATER = F_DEV - TAPS + 1
ALL_VMEM = 40 * 1024 * 1024
BEAM_VMEM = 32 * 1024 * 1024
HEAD = 256
ROWS = 64
MADE = 1024
RING = np.random.RandomState(3).permutation(128).tolist()


def from_behind(block, axis, distance):
    devices = range(lax.axis_size(axis))
    route = [(i - distance, i) for i in devices if i - distance in devices]
    return lax.ppermute(block, axis, route)


def exchange(block):
    return lax.all_to_all(
        block, "gx", split_axis=0, concat_axis=0, axis_index_groups=[RING], tiled=True
    )


def pfb_window():
    total = TAPS * FRAME
    places = np.arange(total, dtype=np.float64)
    centred = (places - (total - 1) * 0.5) / FRAME
    hann = 0.5 - 0.5 * np.cos(2.0 * math.pi * (places + 0.5) / total)
    window = np.sinc(centred) * hann
    window = window * np.sqrt(FRAME / np.sum(window * window))
    return window.reshape(TAPS, FRAME).astype(np.float32)


def folded_table():
    n = np.arange(HALF)
    lane = np.arange(LANES)
    out = np.zeros((BLOCKS, 2, HALF, 2 * LANES), np.float32)
    for block in range(BLOCKS):
        for parity in range(2):
            k = 256 * block + 8 * (lane // 4) + 2 * (lane % 4) + parity
            angle = 2.0 * math.pi / FRAME * (n[:, None] * k[None, :] % FRAME)
            out[block, parity, :, :LANES] = np.cos(angle) / math.sqrt(FRAME)
            out[block, parity, :, LANES:] = -np.sin(angle) / math.sqrt(FRAME)
    return out.astype(jnp.bfloat16)


def gain_select():
    lane = np.arange(LANES)
    out = np.zeros((256, 2 * LANES), np.float32)
    for parity in range(2):
        k = 8 * (lane // 4) + 2 * (lane % 4) + parity
        out[k, parity * LANES + lane] = 1.0
    return out.astype(jnp.bfloat16)


def north_table():
    index = np.arange(FEEDS)
    angle = 2.0 * math.pi / FEEDS * (index[:, None] * index[None, :] % FEEDS)
    scale = 1.0 / math.sqrt(FEEDS)
    table = np.concatenate([np.cos(angle), np.sin(angle)], 0) * scale
    return (table.astype(jnp.bfloat16).astype(np.float32) * 0.5).astype(jnp.bfloat16)


def fine_table():
    scale = 1.0 / math.sqrt(UPCH)
    out = np.zeros((2, F_DEV, 2, 4, 2, CH_DEV, UPCH), np.float32)
    j = np.arange(UPCH)
    angle = 2.0 * math.pi / UPCH * (j[:, None] * j[None, :] % UPCH)
    cosine, sine = np.cos(angle) * scale, np.sin(angle) * scale
    for parity in range(2):
        for h in range(4):
            channel = 2 * h + parity
            out[0, :, parity, h, 0, channel, :] = cosine
            out[0, :, parity, h, 1, channel, :] = -sine
            out[1, :, parity, h, 0, channel, :] = sine
            out[1, :, parity, h, 1, channel, :] = cosine
    return out.reshape(256, 256).astype(jnp.bfloat16)


def swap_groups(arrays):
    lane = lax.broadcasted_iota(jnp.int32, arrays[0].shape, 1) // 4
    arrays = list(arrays)
    bit = len(arrays) // 2
    while bit:
        low = (lane & bit) == 0
        for j in range(len(arrays)):
            if j & bit:
                continue
            a, b = arrays[j], arrays[j | bit]
            arrays[j] = jnp.where(low, a, pltpu.roll(b, 4 * bit, 1))
            arrays[j | bit] = jnp.where(low, pltpu.roll(a, LANES - 4 * bit, 1), b)
        bit //= 2
    return arrays


def filter_frames(frames, w, first, count):
    rows = []
    for f in range(first, first + count):
        total = frames[f - TAPS + 1] * w[0]
        for t in range(1, TAPS):
            total = total + frames[f - TAPS + 1 + t] * w[t]
        rows.append(total)
    return rows


def fold_frames(parts, w_ref, z_ref, count):
    def chunk(c, carry):
        halves = []
        for half in range(2):
            at = pl.multiple_of(half * HALF + c * LANES, LANES)
            w = [w_ref[t : t + 1, pl.ds(at, LANES)] for t in range(TAPS)]
            frames = []
            for ref in parts:
                for f in range(ref.shape[1] // FRAME):
                    frames.append(ref[:, pl.ds(f * FRAME + at, LANES)].astype(jnp.float32))
            halves.append(filter_frames(frames, w, TAPS - 1, count))
        to = pl.ds(pl.multiple_of(c * LANES, LANES), LANES)
        for f in range(count):
            a, b = halves[0][f], halves[1][f]
            z_ref[0, pl.ds(f * IN_DEV, IN_DEV), to] = (a + b).astype(jnp.bfloat16)
            z_ref[1, pl.ds(f * IN_DEV, IN_DEV), to] = (a - b).astype(jnp.bfloat16)
        return carry

    lax.fori_loop(0, HALF // LANES, chunk, 0)


def calibrate(z, table, gain_re, gain_im):
    spectra = jnp.dot(z, table, preferred_element_type=jnp.float32)
    real, imag = [], []
    for f in range(z.shape[0] // IN_DEV):
        s_re = spectra[f * IN_DEV : (f + 1) * IN_DEV, :LANES]
        s_im = spectra[f * IN_DEV : (f + 1) * IN_DEV, LANES:]
        real.append(gain_re * s_re - gain_im * s_im)
        imag.append(gain_re * s_im + gain_im * s_re)
    return real, imag


def later_kernel(
    x_hbm, w_hbm, t_hbm, sel_hbm, g_hbm, x_ref, w_ref, t_ref, out_ref, picked_ref, sel_ref, g_ref, z_ref, sems
):
    copies = [
        pltpu.make_async_copy(x_hbm, x_ref, sems.at[0]),
        pltpu.make_async_copy(w_hbm, w_ref, sems.at[1]),
        pltpu.make_async_copy(sel_hbm, sel_ref, sems.at[2]),
        pltpu.make_async_copy(g_hbm, g_ref, sems.at[3]),
    ]
    for block in range(BLOCKS):
        copies.append(pltpu.make_async_copy(t_hbm.at[block], t_ref.at[block], sems.at[4 + block]))
    for copy in copies:
        copy.start()
    for copy in copies[:2]:
        copy.wait()
    fold_frames([x_ref], w_ref, z_ref, LATER)
    for copy in copies[2:4]:
        copy.wait()
    for block in range(BLOCKS):
        columns = slice(block * 256, (block + 1) * 256)
        g = jnp.concatenate([g_ref[0, :, columns], g_ref[1, :, columns]], 0)
        g_hi = g.astype(jnp.bfloat16)
        rest = g - g_hi.astype(jnp.float32)
        g_mid = rest.astype(jnp.bfloat16)
        g_low = (rest - g_mid.astype(jnp.float32)).astype(jnp.bfloat16)
        parts = jnp.concatenate([g_hi, g_mid, g_low], 0)
        picked = jnp.dot(parts, sel_ref[...], preferred_element_type=jnp.float32)
        picked_ref[block] = picked[0:32] + picked[32:64] + picked[64:96]
    none = jnp.zeros((IN_DEV, LANES), jnp.bfloat16)
    for block in range(BLOCKS):
        copies[4 + block].wait()
        picked = picked_ref[block]
        values = [[none] * 32, [none] * 32]
        for parity in range(2):
            lanes = slice(parity * LANES, (parity + 1) * LANES)
            late = calibrate(
                z_ref[parity], t_ref[block, parity], picked[0:16, lanes], picked[16:32, lanes]
            )
            for part in range(2):
                for f in range(LATER):
                    values[part][2 * (f + TAPS - 1) + parity] = late[part][f].astype(jnp.bfloat16)
        for part in range(2):
            arrays = swap_groups(values[part])
            for d in range(32):
                rows = pl.ds((block * 32 + d) * IN_DEV, IN_DEV)
                out_ref[rows, pl.ds(part * LANES, LANES)] = arrays[d]


def first_kernel(x_ref, prior_ref, w_ref, t_ref, picked_ref, later_ref, out_hbm, z_ref, out_ref, sems):
    fold_frames([prior_ref, x_ref.at[:, : (TAPS - 1) * FRAME]], w_ref, z_ref, TAPS - 1)
    none = jnp.zeros((IN_DEV, LANES), jnp.bfloat16)
    is_early = lax.broadcasted_iota(jnp.int32, (IN_DEV, LANES), 1) < CH_DEV * (TAPS - 1)
    copies = []
    for block in range(BLOCKS):
        picked = picked_ref[block]
        values = [[none] * 8, [none] * 8]
        for parity in range(2):
            lanes = slice(parity * LANES, (parity + 1) * LANES)
            early = calibrate(
                z_ref[parity], t_ref[block, parity], picked[0:16, lanes], picked[16:32, lanes]
            )
            for part in range(2):
                for f in range(TAPS - 1):
                    values[part][2 * f + parity] = early[part][f].astype(jnp.bfloat16)
        for part in range(2):
            arrays = swap_groups(values[part])
            for d in range(32):
                rows = pl.ds((block * 32 + d) * IN_DEV, IN_DEV)
                lanes = pl.ds(part * LANES, LANES)
                moved = arrays[d % 8]
                if d >= 8:
                    moved = pltpu.roll(moved, LANES - 32 * (d // 8), 1)
                out_ref[rows, lanes] = jnp.where(is_early, moved, later_ref[rows, lanes])
        rows = pl.ds(block * 32 * IN_DEV, 32 * IN_DEV)
        copies.append(pltpu.make_async_copy(out_ref.at[rows], out_hbm.at[rows], sems.at[block]))
        copies[block].start()
    for copy in copies:
        copy.wait()


IN_VMEM = pl.BlockSpec(memory_space=pltpu.VMEM)
IN_HBM = pl.BlockSpec(memory_space=pltpu.HBM)


def channelize_later(samples, gains):
    table = folded_table()
    return pl.pallas_call(
        later_kernel,
        in_specs=[IN_HBM] * 5,
        out_specs=[IN_VMEM] * 5,
        out_shape=[
            pltpu.VMEM((IN_DEV, F_DEV * FRAME), jnp.bfloat16),
            pltpu.VMEM((TAPS, FRAME), jnp.float32),
            pltpu.VMEM(table.shape, jnp.bfloat16),
            pltpu.VMEM((INPUTS, 256), jnp.bfloat16),
            pltpu.VMEM((BLOCKS, 2 * IN_DEV, 2 * LANES), jnp.float32),
        ],
        scratch_shapes=[
            pltpu.VMEM((256, 256), jnp.bfloat16),
            pltpu.VMEM((2, IN_DEV, CHANNELS), jnp.float32),
            pltpu.VMEM((2, LATER * IN_DEV, HALF), jnp.bfloat16),
            pltpu.SemaphoreType.DMA((4 + BLOCKS,)),
        ],
        compiler_params=pltpu.CompilerParams(vmem_limit_bytes=ALL_VMEM),
        cost_estimate=pl.CostEstimate(
            flops=2 * 256 * 1024 * 2048, bytes_accessed=7 * 1024 * 1024, transcendentals=0
        ),
        name="channelize_later",
    )(
        *(
            pltpu.with_memory_space_constraint(x, pltpu.HBM)
            for x in (
                samples,
                jnp.asarray(pfb_window()),
                jnp.asarray(table),
                jnp.asarray(gain_select()),
                gains,
            )
        )
    )


def channelize_first(samples, prior, window, table, picked, later):
    return pl.pallas_call(
        first_kernel,
        in_specs=[IN_VMEM] * 6,
        out_specs=IN_HBM,
        out_shape=jax.ShapeDtypeStruct((INPUTS, 256), jnp.bfloat16),
        scratch_shapes=[
            pltpu.VMEM((2, (TAPS - 1) * IN_DEV, HALF), jnp.bfloat16),
            pltpu.VMEM((INPUTS, 256), jnp.bfloat16),
            pltpu.SemaphoreType.DMA((BLOCKS,)),
        ],
        compiler_params=pltpu.CompilerParams(vmem_limit_bytes=BEAM_VMEM),
        cost_estimate=pl.CostEstimate(
            flops=2 * 48 * 1024 * 2048, bytes_accessed=7 * 1024 * 1024, transcendentals=0
        ),
        name="channelize_first",
    )(samples, prior, window, table, picked, later)


def one_hot_kernel(slots_ref, order_ref, ids_ref, head_ref, rest_hbm, turn_hbm, rest_ref, turn_ref, sems):
    slots = jnp.transpose(slots_ref[...])
    copies = []
    for block in [*range(HEAD // LANES), *range(MADE // LANES, INPUTS // LANES)]:
        hot = jnp.where(slots[:, block : block + 1] == ids_ref[...], 1.0, 0.0).astype(jnp.bfloat16)
        at = block * LANES
        if at < HEAD:
            head_ref[pl.ds(at, LANES), :] = hot
            continue
        rows = pl.ds(at - MADE, LANES)
        rest_ref[rows, :] = hot
        copies.append(
            pltpu.make_async_copy(rest_ref.at[rows], rest_hbm.at[rows], sems.at[len(copies)])
        )
        copies[-1].start()
    beams = jnp.transpose(order_ref[...])
    index = lax.broadcasted_iota(jnp.int32, (2 * CH_DEV, BEAMS), 1)
    for pair in range(BEAMS // (2 * CH_DEV)):
        columns = []
        for g in RING[2 * pair : 2 * pair + 2]:
            row = g * CH_DEV % LANES
            at = g * CH_DEV // LANES
            columns.append(beams[row : row + CH_DEV, at : at + 1])
        turn_ref[pl.ds(pair * 2 * CH_DEV, 2 * CH_DEV), :] = jnp.where(
            jnp.concatenate(columns, 0) == index, 1.0, 0.0
        ).astype(jnp.bfloat16)
    copies.append(pltpu.make_async_copy(turn_ref, turn_hbm, sems.at[len(copies)]))
    copies[-1].start()
    for copy in copies:
        copy.wait()


def one_hots(slots, beam_order, ids):
    return pl.pallas_call(
        one_hot_kernel,
        in_specs=[IN_VMEM] * 3,
        out_specs=[IN_VMEM, IN_HBM, IN_HBM],
        out_shape=[
            pltpu.VMEM((HEAD, INPUTS), jnp.bfloat16),
            pltpu.HBM((INPUTS - MADE, INPUTS), jnp.bfloat16),
            pltpu.HBM((BEAMS, BEAMS), jnp.bfloat16),
        ],
        scratch_shapes=[
            pltpu.VMEM((INPUTS - MADE, INPUTS), jnp.bfloat16),
            pltpu.VMEM((BEAMS, BEAMS), jnp.bfloat16),
            pltpu.SemaphoreType.DMA(((INPUTS - MADE) // LANES + 1,)),
        ],
        compiler_params=pltpu.CompilerParams(vmem_limit_bytes=BEAM_VMEM),
        cost_estimate=pl.CostEstimate(
            flops=20 * 1024 * 1024, bytes_accessed=10 * 1024 * 1024, transcendentals=0
        ),
        name="one_hots",
    )(
        slots,
        beam_order.reshape(BEAMS // LANES, LANES),
        ids,
    )


def beam_kernel(
    x_ref,
    head_ref,
    rest_hbm,
    turn_hbm,
    north_ref,
    fine_ref,
    slots_ref,
    ids_ref,
    out_ref,
    made_ref,
    rest_ref,
    turn_ref,
    fed_ref,
    north_out_ref,
    beam_ref,
    power_ref,
    total_ref,
    sems,
):
    rest_copy = pltpu.make_async_copy(rest_hbm, rest_ref, sems.at[0])
    turn_copy = pltpu.make_async_copy(turn_hbm, turn_ref, sems.at[1])
    rest_copy.start()
    turn_copy.start()
    slots = jnp.transpose(slots_ref[...])
    def feed(step):
        at = step * FEEDS
        if at < HEAD:
            pick = head_ref[pl.ds(at, FEEDS), :]
        elif at < MADE:
            for block in range(at // LANES, (at + FEEDS) // LANES):
                made_ref[pl.ds(block * LANES - HEAD, LANES), :] = jnp.where(
                    slots[:, block : block + 1] == ids_ref[...], 1.0, 0.0
                ).astype(jnp.bfloat16)
            pick = made_ref[pl.ds(at - HEAD, FEEDS), :]
        else:
            if at == MADE:
                rest_copy.wait()
            pick = rest_ref[pl.ds(at - MADE, FEEDS), :]
        fed_ref[pl.ds(at, FEEDS), :] = jnp.dot(
            pick, x_ref[...], preferred_element_type=jnp.float32
        ).astype(jnp.bfloat16)

    def north(step):
        rows = pl.ds(step * FEEDS, FEEDS)
        both = jnp.dot(north_ref[...], fed_ref[rows, :], preferred_element_type=jnp.float32)
        north_out_ref[step, 0] = both[:FEEDS, :LANES] + both[FEEDS:, LANES:]
        north_out_ref[step, 1] = both[:FEEDS, LANES:] - both[FEEDS:, :LANES]

    def east(pol, row):
        rows = pl.ds(row, ROWS)
        re = [north_out_ref[pol * CYL + c, 0, rows, :] for c in range(CYL)]
        im = [north_out_ref[pol * CYL + c, 1, rows, :] for c in range(CYL)]
        sum_re, dif_re = re[0] + re[2], re[0] - re[2]
        sum_im, dif_im = im[0] + im[2], im[0] - im[2]
        odd_re, odd_dif_re = re[1] + re[3], re[1] - re[3]
        odd_im, odd_dif_im = im[1] + im[3], im[1] - im[3]
        out = (
            (sum_re + odd_re, sum_im + odd_im),
            (dif_re + odd_dif_im, dif_im - odd_dif_re),
            (sum_re - odd_re, sum_im - odd_im),
            (dif_re - odd_dif_im, dif_im + odd_dif_re),
        )
        for e in range(CYL):
            at = pl.ds(e * FEEDS + row, ROWS)
            beam_ref[at, :LANES] = out[e][0].astype(jnp.bfloat16)
            beam_ref[at, LANES:] = out[e][1].astype(jnp.bfloat16)

    def detect(pol, e):
        rows = pl.ds(e * FEEDS, FEEDS)
        fine = jnp.dot(beam_ref[rows, :], fine_ref[...], preferred_element_type=jnp.float32)
        squares = fine * fine
        power = squares[:, :LANES] + squares[:, LANES:]
        if pol == 0:
            power_ref[rows, :] = power
        else:
            total_ref[rows, :] = (0.25 * (power_ref[rows, :] + power)).astype(jnp.bfloat16)

    for pol in range(POLS):
        for cyl in range(CYL):
            feed(pol * CYL + cyl)
        for cyl in range(CYL):
            north(pol * CYL + cyl)
        for row in range(0, FEEDS, ROWS):
            east(pol, row)
        for e in range(CYL):
            detect(pol, e)
    turn_copy.wait()
    out_ref[...] = jnp.dot(
        turn_ref[...], total_ref[...], preferred_element_type=jnp.float32
    ).astype(jnp.bfloat16)


def form_beams(piece, head, rest, turn, slots, ids):
    return pl.pallas_call(
        beam_kernel,
        in_specs=[IN_VMEM, IN_VMEM, IN_HBM, IN_HBM, IN_VMEM, IN_VMEM, IN_VMEM, IN_VMEM],
        out_specs=IN_VMEM,
        out_shape=jax.ShapeDtypeStruct((BEAMS, LANES), jnp.bfloat16),
        scratch_shapes=[
            pltpu.VMEM((MADE - HEAD, INPUTS), jnp.bfloat16),
            pltpu.VMEM((INPUTS - MADE, INPUTS), jnp.bfloat16),
            pltpu.VMEM((BEAMS, BEAMS), jnp.bfloat16),
            pltpu.VMEM((INPUTS, 256), jnp.bfloat16),
            pltpu.VMEM((POLS * CYL, 2, FEEDS, LANES), jnp.float32),
            pltpu.VMEM((BEAMS, 256), jnp.bfloat16),
            pltpu.VMEM((BEAMS, LANES), jnp.float32),
            pltpu.VMEM((BEAMS, LANES), jnp.bfloat16),
            pltpu.SemaphoreType.DMA((2,)),
        ],
        compiler_params=pltpu.CompilerParams(vmem_limit_bytes=BEAM_VMEM),
        cost_estimate=pl.CostEstimate(
            flops=2 * 1024 * 1024 * 1500, bytes_accessed=12 * 1024 * 1024, transcendentals=0
        ),
        name="form_beams",
    )(
        piece,
        head,
        pltpu.with_memory_space_constraint(rest, pltpu.HBM),
        pltpu.with_memory_space_constraint(turn, pltpu.HBM),
        jnp.asarray(north_table()),
        jnp.asarray(fine_table()),
        slots,
        ids,
    )


def widen_kernel(x_ref, out_ref):
    for g in range(CHANNELS // CH_DEV):
        out_ref[0, :, g * LANES : (g + 1) * LANES] = x_ref[g].astype(jnp.float32)


def widen(power):
    slots = power.shape[0] * CH_DEV // CHANNELS
    return pl.pallas_call(
        widen_kernel,
        out_shape=jax.ShapeDtypeStruct((1, slots, CHANNELS * UPCH), jnp.float32),
        compiler_params=pltpu.CompilerParams(vmem_limit_bytes=BEAM_VMEM),
        name="widen",
    )(power.reshape(CHANNELS // CH_DEV, slots, LANES))


def body(samples, gains, slot_inputs, beam_order):
    tail = samples[:, (F_DEV - TAPS + 1) * FRAME :]
    prior = from_behind(tail, "ta", 1)
    held, window, table, later, picked = channelize_later(samples, gains)
    calibrated = channelize_first(held, prior, window, table, picked, later)
    piece = exchange(calibrated)
    ids = np.concatenate([np.arange(g * IN_DEV, (g + 1) * IN_DEV) for g in RING])
    ids = jnp.asarray(ids[None, :], jnp.int32)
    slots = slot_inputs.reshape(INPUTS // LANES, LANES)
    head, rest, turn = one_hots(slots, beam_order, ids)
    power = form_beams(piece, head, rest, turn, slots, ids)
    owned = exchange(power)
    return widen(owned)


def solution(mesh):
    placed = (P("gx", "ta"), P(None, "gx", None), P(), P())
    return jax.shard_map(
        body, mesh=mesh, in_specs=placed, out_specs=P("ta", "gx", None), check_vma=False
    )
```

```python
import math

import jax
import jax.numpy as jnp
import numpy as np
from jax import lax
from jax.experimental import pallas as pl
from jax.experimental.pallas import tpu as pltpu
from jax.sharding import PartitionSpec as P

CHANNELS = 1024
FRAME = 2 * CHANNELS
HALF = CHANNELS
FEEDS = 256
CYL = 4
POLS = 2
TAPS = 4
UPCH = 16
BEAMS = 1024
INPUTS = 2048
IN_DEV = 16
F_DEV = 16
CH_DEV = 8
BLOCKS = 4
LANES = 128
LATER = F_DEV - TAPS + 1
ALL_VMEM = 40 * 1024 * 1024
BEAM_VMEM = 32 * 1024 * 1024
HEAD = 256
ROWS = 64
MADE = 1024
RING = list(range(INPUTS // IN_DEV))[::-1]


def from_behind(block, axis, distance):
    devices = range(lax.axis_size(axis))
    route = [(i - distance, i) for i in devices if i - distance in devices]
    return lax.ppermute(block, axis, route)


def exchange(block):
    return lax.all_to_all(
        block, "gx", split_axis=0, concat_axis=0, axis_index_groups=[RING], tiled=True
    )


def pfb_window():
    total = TAPS * FRAME
    places = np.arange(total, dtype=np.float64)
    centred = (places - (total - 1) * 0.5) / FRAME
    hann = 0.5 - 0.5 * np.cos(2.0 * math.pi * (places + 0.5) / total)
    window = np.sinc(centred) * hann
    window = window * np.sqrt(FRAME / np.sum(window * window))
    return window.reshape(TAPS, FRAME).astype(np.float32)


def folded_table():
    n = np.arange(HALF)
    lane = np.arange(LANES)
    out = np.zeros((BLOCKS, 2, HALF, 2 * LANES), np.float32)
    for block in range(BLOCKS):
        for parity in range(2):
            k = 256 * block + 8 * (lane // 4) + 2 * (lane % 4) + parity
            angle = 2.0 * math.pi / FRAME * (n[:, None] * k[None, :] % FRAME)
            out[block, parity, :, :LANES] = np.cos(angle) / math.sqrt(FRAME)
            out[block, parity, :, LANES:] = -np.sin(angle) / math.sqrt(FRAME)
    return out.astype(jnp.bfloat16)


def gain_select():
    lane = np.arange(LANES)
    out = np.zeros((256, 2 * LANES), np.float32)
    for parity in range(2):
        k = 8 * (lane // 4) + 2 * (lane % 4) + parity
        out[k, parity * LANES + lane] = 1.0
    return out.astype(jnp.bfloat16)


def north_table():
    index = np.arange(FEEDS)
    angle = 2.0 * math.pi / FEEDS * (index[:, None] * index[None, :] % FEEDS)
    scale = 1.0 / math.sqrt(FEEDS)
    table = np.concatenate([np.cos(angle), np.sin(angle)], 0) * scale
    return (table.astype(jnp.bfloat16).astype(np.float32) * 0.5).astype(jnp.bfloat16)


def fine_table():
    scale = 1.0 / math.sqrt(UPCH)
    out = np.zeros((2, F_DEV, 2, 4, 2, CH_DEV, UPCH), np.float32)
    j = np.arange(UPCH)
    angle = 2.0 * math.pi / UPCH * (j[:, None] * j[None, :] % UPCH)
    cosine, sine = np.cos(angle) * scale, np.sin(angle) * scale
    for parity in range(2):
        for h in range(4):
            channel = 2 * h + parity
            out[0, :, parity, h, 0, channel, :] = cosine
            out[0, :, parity, h, 1, channel, :] = -sine
            out[1, :, parity, h, 0, channel, :] = sine
            out[1, :, parity, h, 1, channel, :] = cosine
    return out.reshape(256, 256).astype(jnp.bfloat16)


def swap_groups(arrays):
    lane = lax.broadcasted_iota(jnp.int32, arrays[0].shape, 1) // 4
    arrays = list(arrays)
    bit = len(arrays) // 2
    while bit:
        low = (lane & bit) == 0
        for j in range(len(arrays)):
            if j & bit:
                continue
            a, b = arrays[j], arrays[j | bit]
            arrays[j] = jnp.where(low, a, pltpu.roll(b, 4 * bit, 1))
            arrays[j | bit] = jnp.where(low, pltpu.roll(a, LANES - 4 * bit, 1), b)
        bit //= 2
    return arrays


def filter_frames(frames, w, first, count):
    rows = []
    for f in range(first, first + count):
        total = frames[f - TAPS + 1] * w[0]
        for t in range(1, TAPS):
            total = total + frames[f - TAPS + 1 + t] * w[t]
        rows.append(total)
    return rows


def fold_frames(parts, w_ref, z_ref, count):
    def chunk(c, carry):
        halves = []
        for half in range(2):
            at = pl.multiple_of(half * HALF + c * LANES, LANES)
            w = [w_ref[t : t + 1, pl.ds(at, LANES)] for t in range(TAPS)]
            frames = []
            for ref in parts:
                for f in range(ref.shape[1] // FRAME):
                    frames.append(ref[:, pl.ds(f * FRAME + at, LANES)].astype(jnp.float32))
            halves.append(filter_frames(frames, w, TAPS - 1, count))
        to = pl.ds(pl.multiple_of(c * LANES, LANES), LANES)
        for f in range(count):
            a, b = halves[0][f], halves[1][f]
            z_ref[0, pl.ds(f * IN_DEV, IN_DEV), to] = (a + b).astype(jnp.bfloat16)
            z_ref[1, pl.ds(f * IN_DEV, IN_DEV), to] = (a - b).astype(jnp.bfloat16)
        return carry

    lax.fori_loop(0, HALF // LANES, chunk, 0)


def calibrate(z, table, gain_re, gain_im):
    spectra = jnp.dot(z, table, preferred_element_type=jnp.float32)
    real, imag = [], []
    for f in range(z.shape[0] // IN_DEV):
        s_re = spectra[f * IN_DEV : (f + 1) * IN_DEV, :LANES]
        s_im = spectra[f * IN_DEV : (f + 1) * IN_DEV, LANES:]
        real.append(gain_re * s_re - gain_im * s_im)
        imag.append(gain_re * s_im + gain_im * s_re)
    return real, imag


def later_kernel(
    x_hbm, w_hbm, t_hbm, sel_hbm, g_hbm, x_ref, w_ref, t_ref, out_ref, picked_ref, sel_ref, g_ref, z_ref, sems
):
    copies = [
        pltpu.make_async_copy(x_hbm, x_ref, sems.at[0]),
        pltpu.make_async_copy(w_hbm, w_ref, sems.at[1]),
        pltpu.make_async_copy(sel_hbm, sel_ref, sems.at[2]),
        pltpu.make_async_copy(g_hbm, g_ref, sems.at[3]),
    ]
    for block in range(BLOCKS):
        copies.append(pltpu.make_async_copy(t_hbm.at[block], t_ref.at[block], sems.at[4 + block]))
    for copy in copies:
        copy.start()
    for copy in copies[:2]:
        copy.wait()
    fold_frames([x_ref], w_ref, z_ref, LATER)
    for copy in copies[2:4]:
        copy.wait()
    for block in range(BLOCKS):
        columns = slice(block * 256, (block + 1) * 256)
        g = jnp.concatenate([g_ref[0, :, columns], g_ref[1, :, columns]], 0)
        g_hi = g.astype(jnp.bfloat16)
        rest = g - g_hi.astype(jnp.float32)
        g_mid = rest.astype(jnp.bfloat16)
        g_low = (rest - g_mid.astype(jnp.float32)).astype(jnp.bfloat16)
        parts = jnp.concatenate([g_hi, g_mid, g_low], 0)
        picked = jnp.dot(parts, sel_ref[...], preferred_element_type=jnp.float32)
        picked_ref[block] = picked[0:32] + picked[32:64] + picked[64:96]
    none = jnp.zeros((IN_DEV, LANES), jnp.bfloat16)
    for block in range(BLOCKS):
        copies[4 + block].wait()
        picked = picked_ref[block]
        values = [[none] * 32, [none] * 32]
        for parity in range(2):
            lanes = slice(parity * LANES, (parity + 1) * LANES)
            late = calibrate(
                z_ref[parity], t_ref[block, parity], picked[0:16, lanes], picked[16:32, lanes]
            )
            for part in range(2):
                for f in range(LATER):
                    values[part][2 * (f + TAPS - 1) + parity] = late[part][f].astype(jnp.bfloat16)
        for part in range(2):
            arrays = swap_groups(values[part])
            for d in range(32):
                rows = pl.ds((block * 32 + d) * IN_DEV, IN_DEV)
                out_ref[rows, pl.ds(part * LANES, LANES)] = arrays[d]


def first_kernel(x_ref, prior_ref, w_ref, t_ref, picked_ref, later_ref, out_hbm, z_ref, out_ref, sems):
    fold_frames([prior_ref, x_ref.at[:, : (TAPS - 1) * FRAME]], w_ref, z_ref, TAPS - 1)
    none = jnp.zeros((IN_DEV, LANES), jnp.bfloat16)
    is_early = lax.broadcasted_iota(jnp.int32, (IN_DEV, LANES), 1) < CH_DEV * (TAPS - 1)
    copies = []
    for block in range(BLOCKS):
        picked = picked_ref[block]
        values = [[none] * 8, [none] * 8]
        for parity in range(2):
            lanes = slice(parity * LANES, (parity + 1) * LANES)
            early = calibrate(
                z_ref[parity], t_ref[block, parity], picked[0:16, lanes], picked[16:32, lanes]
            )
            for part in range(2):
                for f in range(TAPS - 1):
                    values[part][2 * f + parity] = early[part][f].astype(jnp.bfloat16)
        for part in range(2):
            arrays = swap_groups(values[part])
            for d in range(32):
                rows = pl.ds((block * 32 + d) * IN_DEV, IN_DEV)
                lanes = pl.ds(part * LANES, LANES)
                moved = arrays[d % 8]
                if d >= 8:
                    moved = pltpu.roll(moved, LANES - 32 * (d // 8), 1)
                out_ref[rows, lanes] = jnp.where(is_early, moved, later_ref[rows, lanes])
        rows = pl.ds(block * 32 * IN_DEV, 32 * IN_DEV)
        copies.append(pltpu.make_async_copy(out_ref.at[rows], out_hbm.at[rows], sems.at[block]))
        copies[block].start()
    for copy in copies:
        copy.wait()


IN_VMEM = pl.BlockSpec(memory_space=pltpu.VMEM)
IN_HBM = pl.BlockSpec(memory_space=pltpu.HBM)


def channelize_later(samples, gains):
    table = folded_table()
    return pl.pallas_call(
        later_kernel,
        in_specs=[IN_HBM] * 5,
        out_specs=[IN_VMEM] * 5,
        out_shape=[
            pltpu.VMEM((IN_DEV, F_DEV * FRAME), jnp.bfloat16),
            pltpu.VMEM((TAPS, FRAME), jnp.float32),
            pltpu.VMEM(table.shape, jnp.bfloat16),
            pltpu.VMEM((INPUTS, 256), jnp.bfloat16),
            pltpu.VMEM((BLOCKS, 2 * IN_DEV, 2 * LANES), jnp.float32),
        ],
        scratch_shapes=[
            pltpu.VMEM((256, 256), jnp.bfloat16),
            pltpu.VMEM((2, IN_DEV, CHANNELS), jnp.float32),
            pltpu.VMEM((2, LATER * IN_DEV, HALF), jnp.bfloat16),
            pltpu.SemaphoreType.DMA((4 + BLOCKS,)),
        ],
        compiler_params=pltpu.CompilerParams(vmem_limit_bytes=ALL_VMEM),
        cost_estimate=pl.CostEstimate(
            flops=2 * 256 * 1024 * 2048, bytes_accessed=7 * 1024 * 1024, transcendentals=0
        ),
        name="channelize_later",
    )(
        *(
            pltpu.with_memory_space_constraint(x, pltpu.HBM)
            for x in (
                samples,
                jnp.asarray(pfb_window()),
                jnp.asarray(table),
                jnp.asarray(gain_select()),
                gains,
            )
        )
    )


def channelize_first(samples, prior, window, table, picked, later):
    return pl.pallas_call(
        first_kernel,
        in_specs=[IN_VMEM] * 6,
        out_specs=IN_HBM,
        out_shape=jax.ShapeDtypeStruct((INPUTS, 256), jnp.bfloat16),
        scratch_shapes=[
            pltpu.VMEM((2, (TAPS - 1) * IN_DEV, HALF), jnp.bfloat16),
            pltpu.VMEM((INPUTS, 256), jnp.bfloat16),
            pltpu.SemaphoreType.DMA((BLOCKS,)),
        ],
        compiler_params=pltpu.CompilerParams(vmem_limit_bytes=BEAM_VMEM),
        cost_estimate=pl.CostEstimate(
            flops=2 * 48 * 1024 * 2048, bytes_accessed=7 * 1024 * 1024, transcendentals=0
        ),
        name="channelize_first",
    )(samples, prior, window, table, picked, later)


def one_hot_kernel(slots_ref, order_ref, ids_ref, head_ref, rest_hbm, turn_hbm, rest_ref, turn_ref, sems):
    slots = jnp.transpose(slots_ref[...])
    copies = []
    for block in [*range(HEAD // LANES), *range(MADE // LANES, INPUTS // LANES)]:
        hot = jnp.where(slots[:, block : block + 1] == ids_ref[...], 1.0, 0.0).astype(jnp.bfloat16)
        at = block * LANES
        if at < HEAD:
            head_ref[pl.ds(at, LANES), :] = hot
            continue
        rows = pl.ds(at - MADE, LANES)
        rest_ref[rows, :] = hot
        copies.append(
            pltpu.make_async_copy(rest_ref.at[rows], rest_hbm.at[rows], sems.at[len(copies)])
        )
        copies[-1].start()
    beams = jnp.transpose(order_ref[...])
    index = lax.broadcasted_iota(jnp.int32, (2 * CH_DEV, BEAMS), 1)
    for pair in range(BEAMS // (2 * CH_DEV)):
        columns = []
        for g in RING[2 * pair : 2 * pair + 2]:
            row = g * CH_DEV % LANES
            at = g * CH_DEV // LANES
            columns.append(beams[row : row + CH_DEV, at : at + 1])
        turn_ref[pl.ds(pair * 2 * CH_DEV, 2 * CH_DEV), :] = jnp.where(
            jnp.concatenate(columns, 0) == index, 1.0, 0.0
        ).astype(jnp.bfloat16)
    copies.append(pltpu.make_async_copy(turn_ref, turn_hbm, sems.at[len(copies)]))
    copies[-1].start()
    for copy in copies:
        copy.wait()


def one_hots(slots, beam_order, ids):
    return pl.pallas_call(
        one_hot_kernel,
        in_specs=[IN_VMEM] * 3,
        out_specs=[IN_VMEM, IN_HBM, IN_HBM],
        out_shape=[
            pltpu.VMEM((HEAD, INPUTS), jnp.bfloat16),
            pltpu.HBM((INPUTS - MADE, INPUTS), jnp.bfloat16),
            pltpu.HBM((BEAMS, BEAMS), jnp.bfloat16),
        ],
        scratch_shapes=[
            pltpu.VMEM((INPUTS - MADE, INPUTS), jnp.bfloat16),
            pltpu.VMEM((BEAMS, BEAMS), jnp.bfloat16),
            pltpu.SemaphoreType.DMA(((INPUTS - MADE) // LANES + 1,)),
        ],
        compiler_params=pltpu.CompilerParams(vmem_limit_bytes=BEAM_VMEM),
        cost_estimate=pl.CostEstimate(
            flops=20 * 1024 * 1024, bytes_accessed=10 * 1024 * 1024, transcendentals=0
        ),
        name="one_hots",
    )(
        slots,
        beam_order.reshape(BEAMS // LANES, LANES),
        ids,
    )


def beam_kernel(
    x_ref,
    head_ref,
    rest_hbm,
    turn_hbm,
    north_ref,
    fine_ref,
    slots_ref,
    ids_ref,
    out_ref,
    made_ref,
    rest_ref,
    turn_ref,
    fed_ref,
    north_out_ref,
    beam_ref,
    power_ref,
    total_ref,
    sems,
):
    rest_copy = pltpu.make_async_copy(rest_hbm, rest_ref, sems.at[0])
    turn_copy = pltpu.make_async_copy(turn_hbm, turn_ref, sems.at[1])
    rest_copy.start()
    turn_copy.start()
    slots = jnp.transpose(slots_ref[...])
    def feed(step):
        at = step * FEEDS
        if at < HEAD:
            pick = head_ref[pl.ds(at, FEEDS), :]
        elif at < MADE:
            for block in range(at // LANES, (at + FEEDS) // LANES):
                made_ref[pl.ds(block * LANES - HEAD, LANES), :] = jnp.where(
                    slots[:, block : block + 1] == ids_ref[...], 1.0, 0.0
                ).astype(jnp.bfloat16)
            pick = made_ref[pl.ds(at - HEAD, FEEDS), :]
        else:
            if at == MADE:
                rest_copy.wait()
            pick = rest_ref[pl.ds(at - MADE, FEEDS), :]
        fed_ref[pl.ds(at, FEEDS), :] = jnp.dot(
            pick, x_ref[...], preferred_element_type=jnp.float32
        ).astype(jnp.bfloat16)

    def north(step):
        rows = pl.ds(step * FEEDS, FEEDS)
        both = jnp.dot(north_ref[...], fed_ref[rows, :], preferred_element_type=jnp.float32)
        north_out_ref[step, 0] = both[:FEEDS, :LANES] + both[FEEDS:, LANES:]
        north_out_ref[step, 1] = both[:FEEDS, LANES:] - both[FEEDS:, :LANES]

    def east(pol, row):
        rows = pl.ds(row, ROWS)
        re = [north_out_ref[pol * CYL + c, 0, rows, :] for c in range(CYL)]
        im = [north_out_ref[pol * CYL + c, 1, rows, :] for c in range(CYL)]
        sum_re, dif_re = re[0] + re[2], re[0] - re[2]
        sum_im, dif_im = im[0] + im[2], im[0] - im[2]
        odd_re, odd_dif_re = re[1] + re[3], re[1] - re[3]
        odd_im, odd_dif_im = im[1] + im[3], im[1] - im[3]
        out = (
            (sum_re + odd_re, sum_im + odd_im),
            (dif_re + odd_dif_im, dif_im - odd_dif_re),
            (sum_re - odd_re, sum_im - odd_im),
            (dif_re - odd_dif_im, dif_im + odd_dif_re),
        )
        for e in range(CYL):
            at = pl.ds(e * FEEDS + row, ROWS)
            beam_ref[at, :LANES] = out[e][0].astype(jnp.bfloat16)
            beam_ref[at, LANES:] = out[e][1].astype(jnp.bfloat16)

    def detect(pol, e):
        rows = pl.ds(e * FEEDS, FEEDS)
        fine = jnp.dot(beam_ref[rows, :], fine_ref[...], preferred_element_type=jnp.float32)
        squares = fine * fine
        power = squares[:, :LANES] + squares[:, LANES:]
        if pol == 0:
            power_ref[rows, :] = power
        else:
            total_ref[rows, :] = (0.25 * (power_ref[rows, :] + power)).astype(jnp.bfloat16)

    for pol in range(POLS):
        for cyl in range(CYL):
            feed(pol * CYL + cyl)
        for cyl in range(CYL):
            north(pol * CYL + cyl)
        for row in range(0, FEEDS, ROWS):
            east(pol, row)
        for e in range(CYL):
            detect(pol, e)
    turn_copy.wait()
    out_ref[...] = jnp.dot(
        turn_ref[...], total_ref[...], preferred_element_type=jnp.float32
    ).astype(jnp.bfloat16)


def form_beams(piece, head, rest, turn, slots, ids):
    return pl.pallas_call(
        beam_kernel,
        in_specs=[IN_VMEM, IN_VMEM, IN_HBM, IN_HBM, IN_VMEM, IN_VMEM, IN_VMEM, IN_VMEM],
        out_specs=IN_VMEM,
        out_shape=jax.ShapeDtypeStruct((BEAMS, LANES), jnp.bfloat16),
        scratch_shapes=[
            pltpu.VMEM((MADE - HEAD, INPUTS), jnp.bfloat16),
            pltpu.VMEM((INPUTS - MADE, INPUTS), jnp.bfloat16),
            pltpu.VMEM((BEAMS, BEAMS), jnp.bfloat16),
            pltpu.VMEM((INPUTS, 256), jnp.bfloat16),
            pltpu.VMEM((POLS * CYL, 2, FEEDS, LANES), jnp.float32),
            pltpu.VMEM((BEAMS, 256), jnp.bfloat16),
            pltpu.VMEM((BEAMS, LANES), jnp.float32),
            pltpu.VMEM((BEAMS, LANES), jnp.bfloat16),
            pltpu.SemaphoreType.DMA((2,)),
        ],
        compiler_params=pltpu.CompilerParams(vmem_limit_bytes=BEAM_VMEM),
        cost_estimate=pl.CostEstimate(
            flops=2 * 1024 * 1024 * 1500, bytes_accessed=12 * 1024 * 1024, transcendentals=0
        ),
        name="form_beams",
    )(
        piece,
        head,
        pltpu.with_memory_space_constraint(rest, pltpu.HBM),
        pltpu.with_memory_space_constraint(turn, pltpu.HBM),
        jnp.asarray(north_table()),
        jnp.asarray(fine_table()),
        slots,
        ids,
    )


def widen_kernel(x_ref, out_ref):
    for g in range(CHANNELS // CH_DEV):
        out_ref[0, :, g * LANES : (g + 1) * LANES] = x_ref[g].astype(jnp.float32)


def widen(power):
    slots = power.shape[0] * CH_DEV // CHANNELS
    return pl.pallas_call(
        widen_kernel,
        out_shape=jax.ShapeDtypeStruct((1, slots, CHANNELS * UPCH), jnp.float32),
        compiler_params=pltpu.CompilerParams(vmem_limit_bytes=BEAM_VMEM),
        name="widen",
    )(power.reshape(CHANNELS // CH_DEV, slots, LANES))


def body(samples, gains, slot_inputs, beam_order):
    tail = samples[:, (F_DEV - TAPS + 1) * FRAME :]
    prior = from_behind(tail, "ta", 1)
    held, window, table, later, picked = channelize_later(samples, gains)
    calibrated = channelize_first(held, prior, window, table, picked, later)
    piece = exchange(calibrated)
    ids = np.concatenate([np.arange(g * IN_DEV, (g + 1) * IN_DEV) for g in RING])
    ids = jnp.asarray(ids[None, :], jnp.int32)
    slots = slot_inputs.reshape(INPUTS // LANES, LANES)
    head, rest, turn = one_hots(slots, beam_order, ids)
    power = form_beams(piece, head, rest, turn, slots, ids)
    owned = exchange(power)
    return widen(owned)


def solution(mesh):
    placed = (P("gx", "ta"), P(None, "gx", None), P(), P())
    return jax.shard_map(
        body, mesh=mesh, in_specs=placed, out_specs=P("ta", "gx", None), check_vma=False
    )
```

```python
import math

import jax
import jax.numpy as jnp
import numpy as np
from jax import lax
from jax.experimental import pallas as pl
from jax.experimental.pallas import tpu as pltpu
from jax.sharding import PartitionSpec as P

CHANNELS = 1024
FRAME = 2 * CHANNELS
HALF = CHANNELS
FEEDS = 256
CYL = 4
POLS = 2
TAPS = 4
UPCH = 16
BEAMS = 1024
INPUTS = 2048
IN_DEV = 16
F_DEV = 16
CH_DEV = 8
BLOCKS = 4
LANES = 128
LATER = F_DEV - TAPS + 1
ALL_VMEM = 40 * 1024 * 1024
BEAM_VMEM = 32 * 1024 * 1024
HEAD = 256
ROWS = 64
MADE = 1024
RING = [x * 32 + z * 4 + k for x in (3, 2, 1, 0) for z in (7, 3, 6, 2, 5, 1, 4, 0) for k in (3, 2, 1, 0)]


def from_behind(block, axis, distance):
    devices = range(lax.axis_size(axis))
    route = [(i - distance, i) for i in devices if i - distance in devices]
    return lax.ppermute(block, axis, route)


def exchange(block):
    return lax.all_to_all(
        block, "gx", split_axis=0, concat_axis=0, axis_index_groups=[RING], tiled=True
    )


def pfb_window():
    total = TAPS * FRAME
    places = np.arange(total, dtype=np.float64)
    centred = (places - (total - 1) * 0.5) / FRAME
    hann = 0.5 - 0.5 * np.cos(2.0 * math.pi * (places + 0.5) / total)
    window = np.sinc(centred) * hann
    window = window * np.sqrt(FRAME / np.sum(window * window))
    return window.reshape(TAPS, FRAME).astype(np.float32)


def folded_table():
    n = np.arange(HALF)
    lane = np.arange(LANES)
    out = np.zeros((BLOCKS, 2, HALF, 2 * LANES), np.float32)
    for block in range(BLOCKS):
        for parity in range(2):
            k = 256 * block + 8 * (lane // 4) + 2 * (lane % 4) + parity
            angle = 2.0 * math.pi / FRAME * (n[:, None] * k[None, :] % FRAME)
            out[block, parity, :, :LANES] = np.cos(angle) / math.sqrt(FRAME)
            out[block, parity, :, LANES:] = -np.sin(angle) / math.sqrt(FRAME)
    return out.astype(jnp.bfloat16)


def gain_select():
    lane = np.arange(LANES)
    out = np.zeros((256, 2 * LANES), np.float32)
    for parity in range(2):
        k = 8 * (lane // 4) + 2 * (lane % 4) + parity
        out[k, parity * LANES + lane] = 1.0
    return out.astype(jnp.bfloat16)


def north_table():
    index = np.arange(FEEDS)
    angle = 2.0 * math.pi / FEEDS * (index[:, None] * index[None, :] % FEEDS)
    scale = 1.0 / math.sqrt(FEEDS)
    table = np.concatenate([np.cos(angle), np.sin(angle)], 0) * scale
    return (table.astype(jnp.bfloat16).astype(np.float32) * 0.5).astype(jnp.bfloat16)


def fine_table():
    scale = 1.0 / math.sqrt(UPCH)
    out = np.zeros((2, F_DEV, 2, 4, 2, CH_DEV, UPCH), np.float32)
    j = np.arange(UPCH)
    angle = 2.0 * math.pi / UPCH * (j[:, None] * j[None, :] % UPCH)
    cosine, sine = np.cos(angle) * scale, np.sin(angle) * scale
    for parity in range(2):
        for h in range(4):
            channel = 2 * h + parity
            out[0, :, parity, h, 0, channel, :] = cosine
            out[0, :, parity, h, 1, channel, :] = -sine
            out[1, :, parity, h, 0, channel, :] = sine
            out[1, :, parity, h, 1, channel, :] = cosine
    return out.reshape(256, 256).astype(jnp.bfloat16)


def swap_groups(arrays):
    lane = lax.broadcasted_iota(jnp.int32, arrays[0].shape, 1) // 4
    arrays = list(arrays)
    bit = len(arrays) // 2
    while bit:
        low = (lane & bit) == 0
        for j in range(len(arrays)):
            if j & bit:
                continue
            a, b = arrays[j], arrays[j | bit]
            arrays[j] = jnp.where(low, a, pltpu.roll(b, 4 * bit, 1))
            arrays[j | bit] = jnp.where(low, pltpu.roll(a, LANES - 4 * bit, 1), b)
        bit //= 2
    return arrays


def filter_frames(frames, w, first, count):
    rows = []
    for f in range(first, first + count):
        total = frames[f - TAPS + 1] * w[0]
        for t in range(1, TAPS):
            total = total + frames[f - TAPS + 1 + t] * w[t]
        rows.append(total)
    return rows


def fold_frames(parts, w_ref, z_ref, count):
    def chunk(c, carry):
        halves = []
        for half in range(2):
            at = pl.multiple_of(half * HALF + c * LANES, LANES)
            w = [w_ref[t : t + 1, pl.ds(at, LANES)] for t in range(TAPS)]
            frames = []
            for ref in parts:
                for f in range(ref.shape[1] // FRAME):
                    frames.append(ref[:, pl.ds(f * FRAME + at, LANES)].astype(jnp.float32))
            halves.append(filter_frames(frames, w, TAPS - 1, count))
        to = pl.ds(pl.multiple_of(c * LANES, LANES), LANES)
        for f in range(count):
            a, b = halves[0][f], halves[1][f]
            z_ref[0, pl.ds(f * IN_DEV, IN_DEV), to] = (a + b).astype(jnp.bfloat16)
            z_ref[1, pl.ds(f * IN_DEV, IN_DEV), to] = (a - b).astype(jnp.bfloat16)
        return carry

    lax.fori_loop(0, HALF // LANES, chunk, 0)


def calibrate(z, table, gain_re, gain_im):
    spectra = jnp.dot(z, table, preferred_element_type=jnp.float32)
    real, imag = [], []
    for f in range(z.shape[0] // IN_DEV):
        s_re = spectra[f * IN_DEV : (f + 1) * IN_DEV, :LANES]
        s_im = spectra[f * IN_DEV : (f + 1) * IN_DEV, LANES:]
        real.append(gain_re * s_re - gain_im * s_im)
        imag.append(gain_re * s_im + gain_im * s_re)
    return real, imag


def later_kernel(
    x_hbm, w_hbm, t_hbm, sel_hbm, g_hbm, x_ref, w_ref, t_ref, out_ref, picked_ref, sel_ref, g_ref, z_ref, sems
):
    copies = [
        pltpu.make_async_copy(x_hbm, x_ref, sems.at[0]),
        pltpu.make_async_copy(w_hbm, w_ref, sems.at[1]),
        pltpu.make_async_copy(sel_hbm, sel_ref, sems.at[2]),
        pltpu.make_async_copy(g_hbm, g_ref, sems.at[3]),
    ]
    for block in range(BLOCKS):
        copies.append(pltpu.make_async_copy(t_hbm.at[block], t_ref.at[block], sems.at[4 + block]))
    for copy in copies:
        copy.start()
    for copy in copies[:2]:
        copy.wait()
    fold_frames([x_ref], w_ref, z_ref, LATER)
    for copy in copies[2:4]:
        copy.wait()
    for block in range(BLOCKS):
        columns = slice(block * 256, (block + 1) * 256)
        g = jnp.concatenate([g_ref[0, :, columns], g_ref[1, :, columns]], 0)
        g_hi = g.astype(jnp.bfloat16)
        rest = g - g_hi.astype(jnp.float32)
        g_mid = rest.astype(jnp.bfloat16)
        g_low = (rest - g_mid.astype(jnp.float32)).astype(jnp.bfloat16)
        parts = jnp.concatenate([g_hi, g_mid, g_low], 0)
        picked = jnp.dot(parts, sel_ref[...], preferred_element_type=jnp.float32)
        picked_ref[block] = picked[0:32] + picked[32:64] + picked[64:96]
    none = jnp.zeros((IN_DEV, LANES), jnp.bfloat16)
    for block in range(BLOCKS):
        copies[4 + block].wait()
        picked = picked_ref[block]
        values = [[none] * 32, [none] * 32]
        for parity in range(2):
            lanes = slice(parity * LANES, (parity + 1) * LANES)
            late = calibrate(
                z_ref[parity], t_ref[block, parity], picked[0:16, lanes], picked[16:32, lanes]
            )
            for part in range(2):
                for f in range(LATER):
                    values[part][2 * (f + TAPS - 1) + parity] = late[part][f].astype(jnp.bfloat16)
        for part in range(2):
            arrays = swap_groups(values[part])
            for d in range(32):
                rows = pl.ds((block * 32 + d) * IN_DEV, IN_DEV)
                out_ref[rows, pl.ds(part * LANES, LANES)] = arrays[d]


def first_kernel(x_ref, prior_ref, w_ref, t_ref, picked_ref, later_ref, out_hbm, z_ref, out_ref, sems):
    fold_frames([prior_ref, x_ref.at[:, : (TAPS - 1) * FRAME]], w_ref, z_ref, TAPS - 1)
    none = jnp.zeros((IN_DEV, LANES), jnp.bfloat16)
    is_early = lax.broadcasted_iota(jnp.int32, (IN_DEV, LANES), 1) < CH_DEV * (TAPS - 1)
    copies = []
    for block in range(BLOCKS):
        picked = picked_ref[block]
        values = [[none] * 8, [none] * 8]
        for parity in range(2):
            lanes = slice(parity * LANES, (parity + 1) * LANES)
            early = calibrate(
                z_ref[parity], t_ref[block, parity], picked[0:16, lanes], picked[16:32, lanes]
            )
            for part in range(2):
                for f in range(TAPS - 1):
                    values[part][2 * f + parity] = early[part][f].astype(jnp.bfloat16)
        for part in range(2):
            arrays = swap_groups(values[part])
            for d in range(32):
                rows = pl.ds((block * 32 + d) * IN_DEV, IN_DEV)
                lanes = pl.ds(part * LANES, LANES)
                moved = arrays[d % 8]
                if d >= 8:
                    moved = pltpu.roll(moved, LANES - 32 * (d // 8), 1)
                out_ref[rows, lanes] = jnp.where(is_early, moved, later_ref[rows, lanes])
        rows = pl.ds(block * 32 * IN_DEV, 32 * IN_DEV)
        copies.append(pltpu.make_async_copy(out_ref.at[rows], out_hbm.at[rows], sems.at[block]))
        copies[block].start()
    for copy in copies:
        copy.wait()


IN_VMEM = pl.BlockSpec(memory_space=pltpu.VMEM)
IN_HBM = pl.BlockSpec(memory_space=pltpu.HBM)


def channelize_later(samples, gains):
    table = folded_table()
    return pl.pallas_call(
        later_kernel,
        in_specs=[IN_HBM] * 5,
        out_specs=[IN_VMEM] * 5,
        out_shape=[
            pltpu.VMEM((IN_DEV, F_DEV * FRAME), jnp.bfloat16),
            pltpu.VMEM((TAPS, FRAME), jnp.float32),
            pltpu.VMEM(table.shape, jnp.bfloat16),
            pltpu.VMEM((INPUTS, 256), jnp.bfloat16),
            pltpu.VMEM((BLOCKS, 2 * IN_DEV, 2 * LANES), jnp.float32),
        ],
        scratch_shapes=[
            pltpu.VMEM((256, 256), jnp.bfloat16),
            pltpu.VMEM((2, IN_DEV, CHANNELS), jnp.float32),
            pltpu.VMEM((2, LATER * IN_DEV, HALF), jnp.bfloat16),
            pltpu.SemaphoreType.DMA((4 + BLOCKS,)),
        ],
        compiler_params=pltpu.CompilerParams(vmem_limit_bytes=ALL_VMEM),
        cost_estimate=pl.CostEstimate(
            flops=2 * 256 * 1024 * 2048, bytes_accessed=7 * 1024 * 1024, transcendentals=0
        ),
        name="channelize_later",
    )(
        *(
            pltpu.with_memory_space_constraint(x, pltpu.HBM)
            for x in (
                samples,
                jnp.asarray(pfb_window()),
                jnp.asarray(table),
                jnp.asarray(gain_select()),
                gains,
            )
        )
    )


def channelize_first(samples, prior, window, table, picked, later):
    return pl.pallas_call(
        first_kernel,
        in_specs=[IN_VMEM] * 6,
        out_specs=IN_HBM,
        out_shape=jax.ShapeDtypeStruct((INPUTS, 256), jnp.bfloat16),
        scratch_shapes=[
            pltpu.VMEM((2, (TAPS - 1) * IN_DEV, HALF), jnp.bfloat16),
            pltpu.VMEM((INPUTS, 256), jnp.bfloat16),
            pltpu.SemaphoreType.DMA((BLOCKS,)),
        ],
        compiler_params=pltpu.CompilerParams(vmem_limit_bytes=BEAM_VMEM),
        cost_estimate=pl.CostEstimate(
            flops=2 * 48 * 1024 * 2048, bytes_accessed=7 * 1024 * 1024, transcendentals=0
        ),
        name="channelize_first",
    )(samples, prior, window, table, picked, later)


def one_hot_kernel(slots_ref, order_ref, ids_ref, head_ref, rest_hbm, turn_hbm, rest_ref, turn_ref, sems):
    slots = jnp.transpose(slots_ref[...])
    copies = []
    for block in [*range(HEAD // LANES), *range(MADE // LANES, INPUTS // LANES)]:
        hot = jnp.where(slots[:, block : block + 1] == ids_ref[...], 1.0, 0.0).astype(jnp.bfloat16)
        at = block * LANES
        if at < HEAD:
            head_ref[pl.ds(at, LANES), :] = hot
            continue
        rows = pl.ds(at - MADE, LANES)
        rest_ref[rows, :] = hot
        copies.append(
            pltpu.make_async_copy(rest_ref.at[rows], rest_hbm.at[rows], sems.at[len(copies)])
        )
        copies[-1].start()
    beams = jnp.transpose(order_ref[...])
    index = lax.broadcasted_iota(jnp.int32, (2 * CH_DEV, BEAMS), 1)
    for pair in range(BEAMS // (2 * CH_DEV)):
        columns = []
        for g in RING[2 * pair : 2 * pair + 2]:
            row = g * CH_DEV % LANES
            at = g * CH_DEV // LANES
            columns.append(beams[row : row + CH_DEV, at : at + 1])
        turn_ref[pl.ds(pair * 2 * CH_DEV, 2 * CH_DEV), :] = jnp.where(
            jnp.concatenate(columns, 0) == index, 1.0, 0.0
        ).astype(jnp.bfloat16)
    copies.append(pltpu.make_async_copy(turn_ref, turn_hbm, sems.at[len(copies)]))
    copies[-1].start()
    for copy in copies:
        copy.wait()


def one_hots(slots, beam_order, ids):
    return pl.pallas_call(
        one_hot_kernel,
        in_specs=[IN_VMEM] * 3,
        out_specs=[IN_VMEM, IN_HBM, IN_HBM],
        out_shape=[
            pltpu.VMEM((HEAD, INPUTS), jnp.bfloat16),
            pltpu.HBM((INPUTS - MADE, INPUTS), jnp.bfloat16),
            pltpu.HBM((BEAMS, BEAMS), jnp.bfloat16),
        ],
        scratch_shapes=[
            pltpu.VMEM((INPUTS - MADE, INPUTS), jnp.bfloat16),
            pltpu.VMEM((BEAMS, BEAMS), jnp.bfloat16),
            pltpu.SemaphoreType.DMA(((INPUTS - MADE) // LANES + 1,)),
        ],
        compiler_params=pltpu.CompilerParams(vmem_limit_bytes=BEAM_VMEM),
        cost_estimate=pl.CostEstimate(
            flops=20 * 1024 * 1024, bytes_accessed=10 * 1024 * 1024, transcendentals=0
        ),
        name="one_hots",
    )(
        slots,
        beam_order.reshape(BEAMS // LANES, LANES),
        ids,
    )


def beam_kernel(
    x_ref,
    head_ref,
    rest_hbm,
    turn_hbm,
    north_ref,
    fine_ref,
    slots_ref,
    ids_ref,
    out_ref,
    made_ref,
    rest_ref,
    turn_ref,
    fed_ref,
    north_out_ref,
    beam_ref,
    power_ref,
    total_ref,
    sems,
):
    rest_copy = pltpu.make_async_copy(rest_hbm, rest_ref, sems.at[0])
    turn_copy = pltpu.make_async_copy(turn_hbm, turn_ref, sems.at[1])
    rest_copy.start()
    turn_copy.start()
    slots = jnp.transpose(slots_ref[...])
    def feed(step):
        at = step * FEEDS
        if at < HEAD:
            pick = head_ref[pl.ds(at, FEEDS), :]
        elif at < MADE:
            for block in range(at // LANES, (at + FEEDS) // LANES):
                made_ref[pl.ds(block * LANES - HEAD, LANES), :] = jnp.where(
                    slots[:, block : block + 1] == ids_ref[...], 1.0, 0.0
                ).astype(jnp.bfloat16)
            pick = made_ref[pl.ds(at - HEAD, FEEDS), :]
        else:
            if at == MADE:
                rest_copy.wait()
            pick = rest_ref[pl.ds(at - MADE, FEEDS), :]
        fed_ref[pl.ds(at, FEEDS), :] = jnp.dot(
            pick, x_ref[...], preferred_element_type=jnp.float32
        ).astype(jnp.bfloat16)

    def north(step):
        rows = pl.ds(step * FEEDS, FEEDS)
        both = jnp.dot(north_ref[...], fed_ref[rows, :], preferred_element_type=jnp.float32)
        north_out_ref[step, 0] = both[:FEEDS, :LANES] + both[FEEDS:, LANES:]
        north_out_ref[step, 1] = both[:FEEDS, LANES:] - both[FEEDS:, :LANES]

    def east(pol, row):
        rows = pl.ds(row, ROWS)
        re = [north_out_ref[pol * CYL + c, 0, rows, :] for c in range(CYL)]
        im = [north_out_ref[pol * CYL + c, 1, rows, :] for c in range(CYL)]
        sum_re, dif_re = re[0] + re[2], re[0] - re[2]
        sum_im, dif_im = im[0] + im[2], im[0] - im[2]
        odd_re, odd_dif_re = re[1] + re[3], re[1] - re[3]
        odd_im, odd_dif_im = im[1] + im[3], im[1] - im[3]
        out = (
            (sum_re + odd_re, sum_im + odd_im),
            (dif_re + odd_dif_im, dif_im - odd_dif_re),
            (sum_re - odd_re, sum_im - odd_im),
            (dif_re - odd_dif_im, dif_im + odd_dif_re),
        )
        for e in range(CYL):
            at = pl.ds(e * FEEDS + row, ROWS)
            beam_ref[at, :LANES] = out[e][0].astype(jnp.bfloat16)
            beam_ref[at, LANES:] = out[e][1].astype(jnp.bfloat16)

    def detect(pol, e):
        rows = pl.ds(e * FEEDS, FEEDS)
        fine = jnp.dot(beam_ref[rows, :], fine_ref[...], preferred_element_type=jnp.float32)
        squares = fine * fine
        power = squares[:, :LANES] + squares[:, LANES:]
        if pol == 0:
            power_ref[rows, :] = power
        else:
            total_ref[rows, :] = (0.25 * (power_ref[rows, :] + power)).astype(jnp.bfloat16)

    for pol in range(POLS):
        for cyl in range(CYL):
            feed(pol * CYL + cyl)
        for cyl in range(CYL):
            north(pol * CYL + cyl)
        for row in range(0, FEEDS, ROWS):
            east(pol, row)
        for e in range(CYL):
            detect(pol, e)
    turn_copy.wait()
    out_ref[...] = jnp.dot(
        turn_ref[...], total_ref[...], preferred_element_type=jnp.float32
    ).astype(jnp.bfloat16)


def form_beams(piece, head, rest, turn, slots, ids):
    return pl.pallas_call(
        beam_kernel,
        in_specs=[IN_VMEM, IN_VMEM, IN_HBM, IN_HBM, IN_VMEM, IN_VMEM, IN_VMEM, IN_VMEM],
        out_specs=IN_VMEM,
        out_shape=jax.ShapeDtypeStruct((BEAMS, LANES), jnp.bfloat16),
        scratch_shapes=[
            pltpu.VMEM((MADE - HEAD, INPUTS), jnp.bfloat16),
            pltpu.VMEM((INPUTS - MADE, INPUTS), jnp.bfloat16),
            pltpu.VMEM((BEAMS, BEAMS), jnp.bfloat16),
            pltpu.VMEM((INPUTS, 256), jnp.bfloat16),
            pltpu.VMEM((POLS * CYL, 2, FEEDS, LANES), jnp.float32),
            pltpu.VMEM((BEAMS, 256), jnp.bfloat16),
            pltpu.VMEM((BEAMS, LANES), jnp.float32),
            pltpu.VMEM((BEAMS, LANES), jnp.bfloat16),
            pltpu.SemaphoreType.DMA((2,)),
        ],
        compiler_params=pltpu.CompilerParams(vmem_limit_bytes=BEAM_VMEM),
        cost_estimate=pl.CostEstimate(
            flops=2 * 1024 * 1024 * 1500, bytes_accessed=12 * 1024 * 1024, transcendentals=0
        ),
        name="form_beams",
    )(
        piece,
        head,
        pltpu.with_memory_space_constraint(rest, pltpu.HBM),
        pltpu.with_memory_space_constraint(turn, pltpu.HBM),
        jnp.asarray(north_table()),
        jnp.asarray(fine_table()),
        slots,
        ids,
    )


def widen_kernel(x_ref, out_ref):
    for g in range(CHANNELS // CH_DEV):
        out_ref[0, :, g * LANES : (g + 1) * LANES] = x_ref[g].astype(jnp.float32)


def widen(power):
    slots = power.shape[0] * CH_DEV // CHANNELS
    return pl.pallas_call(
        widen_kernel,
        out_shape=jax.ShapeDtypeStruct((1, slots, CHANNELS * UPCH), jnp.float32),
        compiler_params=pltpu.CompilerParams(vmem_limit_bytes=BEAM_VMEM),
        name="widen",
    )(power.reshape(CHANNELS // CH_DEV, slots, LANES))


def body(samples, gains, slot_inputs, beam_order):
    tail = samples[:, (F_DEV - TAPS + 1) * FRAME :]
    prior = from_behind(tail, "ta", 1)
    held, window, table, later, picked = channelize_later(samples, gains)
    calibrated = channelize_first(held, prior, window, table, picked, later)
    piece = exchange(calibrated)
    ids = np.concatenate([np.arange(g * IN_DEV, (g + 1) * IN_DEV) for g in RING])
    ids = jnp.asarray(ids[None, :], jnp.int32)
    slots = slot_inputs.reshape(INPUTS // LANES, LANES)
    head, rest, turn = one_hots(slots, beam_order, ids)
    power = form_beams(piece, head, rest, turn, slots, ids)
    owned = exchange(power)
    return widen(owned)


def solution(mesh):
    placed = (P("gx", "ta"), P(None, "gx", None), P(), P())
    return jax.shard_map(
        body, mesh=mesh, in_specs=placed, out_specs=P("ta", "gx", None), check_vma=False
    )
```

```python
import math

import jax
import jax.numpy as jnp
import numpy as np
from jax import lax
from jax.experimental import pallas as pl
from jax.experimental.pallas import tpu as pltpu
from jax.sharding import PartitionSpec as P

CHANNELS = 1024
FRAME = 2 * CHANNELS
HALF = CHANNELS
FEEDS = 256
CYL = 4
POLS = 2
TAPS = 4
UPCH = 16
BEAMS = 1024
INPUTS = 2048
IN_DEV = 16
F_DEV = 16
CH_DEV = 8
BLOCKS = 4
LANES = 128
LATER = F_DEV - TAPS + 1
ALL_VMEM = 40 * 1024 * 1024
BEAM_VMEM = 32 * 1024 * 1024
HEAD = 256
ROWS = 64
MADE = 1024
RING = [x * 32 + z * 4 + k for zs in ((7, 3), (6, 2), (5, 1), (4, 0)) for x in (3, 2, 1, 0) for z in zs for k in (3, 2, 1, 0)]


def from_behind(block, axis, distance):
    devices = range(lax.axis_size(axis))
    route = [(i - distance, i) for i in devices if i - distance in devices]
    return lax.ppermute(block, axis, route)


def exchange(block):
    return lax.all_to_all(
        block, "gx", split_axis=0, concat_axis=0, axis_index_groups=[RING], tiled=True
    )


def pfb_window():
    total = TAPS * FRAME
    places = np.arange(total, dtype=np.float64)
    centred = (places - (total - 1) * 0.5) / FRAME
    hann = 0.5 - 0.5 * np.cos(2.0 * math.pi * (places + 0.5) / total)
    window = np.sinc(centred) * hann
    window = window * np.sqrt(FRAME / np.sum(window * window))
    return window.reshape(TAPS, FRAME).astype(np.float32)


def folded_table():
    n = np.arange(HALF)
    lane = np.arange(LANES)
    out = np.zeros((BLOCKS, 2, HALF, 2 * LANES), np.float32)
    for block in range(BLOCKS):
        for parity in range(2):
            k = 256 * block + 8 * (lane // 4) + 2 * (lane % 4) + parity
            angle = 2.0 * math.pi / FRAME * (n[:, None] * k[None, :] % FRAME)
            out[block, parity, :, :LANES] = np.cos(angle) / math.sqrt(FRAME)
            out[block, parity, :, LANES:] = -np.sin(angle) / math.sqrt(FRAME)
    return out.astype(jnp.bfloat16)


def gain_select():
    lane = np.arange(LANES)
    out = np.zeros((256, 2 * LANES), np.float32)
    for parity in range(2):
        k = 8 * (lane // 4) + 2 * (lane % 4) + parity
        out[k, parity * LANES + lane] = 1.0
    return out.astype(jnp.bfloat16)


def north_table():
    index = np.arange(FEEDS)
    angle = 2.0 * math.pi / FEEDS * (index[:, None] * index[None, :] % FEEDS)
    scale = 1.0 / math.sqrt(FEEDS)
    table = np.concatenate([np.cos(angle), np.sin(angle)], 0) * scale
    return (table.astype(jnp.bfloat16).astype(np.float32) * 0.5).astype(jnp.bfloat16)


def fine_table():
    scale = 1.0 / math.sqrt(UPCH)
    out = np.zeros((2, F_DEV, 2, 4, 2, CH_DEV, UPCH), np.float32)
    j = np.arange(UPCH)
    angle = 2.0 * math.pi / UPCH * (j[:, None] * j[None, :] % UPCH)
    cosine, sine = np.cos(angle) * scale, np.sin(angle) * scale
    for parity in range(2):
        for h in range(4):
            channel = 2 * h + parity
            out[0, :, parity, h, 0, channel, :] = cosine
            out[0, :, parity, h, 1, channel, :] = -sine
            out[1, :, parity, h, 0, channel, :] = sine
            out[1, :, parity, h, 1, channel, :] = cosine
    return out.reshape(256, 256).astype(jnp.bfloat16)


def swap_groups(arrays):
    lane = lax.broadcasted_iota(jnp.int32, arrays[0].shape, 1) // 4
    arrays = list(arrays)
    bit = len(arrays) // 2
    while bit:
        low = (lane & bit) == 0
        for j in range(len(arrays)):
            if j & bit:
                continue
            a, b = arrays[j], arrays[j | bit]
            arrays[j] = jnp.where(low, a, pltpu.roll(b, 4 * bit, 1))
            arrays[j | bit] = jnp.where(low, pltpu.roll(a, LANES - 4 * bit, 1), b)
        bit //= 2
    return arrays


def filter_frames(frames, w, first, count):
    rows = []
    for f in range(first, first + count):
        total = frames[f - TAPS + 1] * w[0]
        for t in range(1, TAPS):
            total = total + frames[f - TAPS + 1 + t] * w[t]
        rows.append(total)
    return rows


def fold_frames(parts, w_ref, z_ref, count):
    def chunk(c, carry):
        halves = []
        for half in range(2):
            at = pl.multiple_of(half * HALF + c * LANES, LANES)
            w = [w_ref[t : t + 1, pl.ds(at, LANES)] for t in range(TAPS)]
            frames = []
            for ref in parts:
                for f in range(ref.shape[1] // FRAME):
                    frames.append(ref[:, pl.ds(f * FRAME + at, LANES)].astype(jnp.float32))
            halves.append(filter_frames(frames, w, TAPS - 1, count))
        to = pl.ds(pl.multiple_of(c * LANES, LANES), LANES)
        for f in range(count):
            a, b = halves[0][f], halves[1][f]
            z_ref[0, pl.ds(f * IN_DEV, IN_DEV), to] = (a + b).astype(jnp.bfloat16)
            z_ref[1, pl.ds(f * IN_DEV, IN_DEV), to] = (a - b).astype(jnp.bfloat16)
        return carry

    lax.fori_loop(0, HALF // LANES, chunk, 0)


def calibrate(z, table, gain_re, gain_im):
    spectra = jnp.dot(z, table, preferred_element_type=jnp.float32)
    real, imag = [], []
    for f in range(z.shape[0] // IN_DEV):
        s_re = spectra[f * IN_DEV : (f + 1) * IN_DEV, :LANES]
        s_im = spectra[f * IN_DEV : (f + 1) * IN_DEV, LANES:]
        real.append(gain_re * s_re - gain_im * s_im)
        imag.append(gain_re * s_im + gain_im * s_re)
    return real, imag


def later_kernel(
    x_hbm, w_hbm, t_hbm, sel_hbm, g_hbm, x_ref, w_ref, t_ref, out_ref, picked_ref, sel_ref, g_ref, z_ref, sems
):
    copies = [
        pltpu.make_async_copy(x_hbm, x_ref, sems.at[0]),
        pltpu.make_async_copy(w_hbm, w_ref, sems.at[1]),
        pltpu.make_async_copy(sel_hbm, sel_ref, sems.at[2]),
        pltpu.make_async_copy(g_hbm, g_ref, sems.at[3]),
    ]
    for block in range(BLOCKS):
        copies.append(pltpu.make_async_copy(t_hbm.at[block], t_ref.at[block], sems.at[4 + block]))
    for copy in copies:
        copy.start()
    for copy in copies[:2]:
        copy.wait()
    fold_frames([x_ref], w_ref, z_ref, LATER)
    for copy in copies[2:4]:
        copy.wait()
    for block in range(BLOCKS):
        columns = slice(block * 256, (block + 1) * 256)
        g = jnp.concatenate([g_ref[0, :, columns], g_ref[1, :, columns]], 0)
        g_hi = g.astype(jnp.bfloat16)
        rest = g - g_hi.astype(jnp.float32)
        g_mid = rest.astype(jnp.bfloat16)
        g_low = (rest - g_mid.astype(jnp.float32)).astype(jnp.bfloat16)
        parts = jnp.concatenate([g_hi, g_mid, g_low], 0)
        picked = jnp.dot(parts, sel_ref[...], preferred_element_type=jnp.float32)
        picked_ref[block] = picked[0:32] + picked[32:64] + picked[64:96]
    none = jnp.zeros((IN_DEV, LANES), jnp.bfloat16)
    for block in range(BLOCKS):
        copies[4 + block].wait()
        picked = picked_ref[block]
        values = [[none] * 32, [none] * 32]
        for parity in range(2):
            lanes = slice(parity * LANES, (parity + 1) * LANES)
            late = calibrate(
                z_ref[parity], t_ref[block, parity], picked[0:16, lanes], picked[16:32, lanes]
            )
            for part in range(2):
                for f in range(LATER):
                    values[part][2 * (f + TAPS - 1) + parity] = late[part][f].astype(jnp.bfloat16)
        for part in range(2):
            arrays = swap_groups(values[part])
            for d in range(32):
                rows = pl.ds((block * 32 + d) * IN_DEV, IN_DEV)
                out_ref[rows, pl.ds(part * LANES, LANES)] = arrays[d]


def first_kernel(x_ref, prior_ref, w_ref, t_ref, picked_ref, later_ref, out_hbm, z_ref, out_ref, sems):
    fold_frames([prior_ref, x_ref.at[:, : (TAPS - 1) * FRAME]], w_ref, z_ref, TAPS - 1)
    none = jnp.zeros((IN_DEV, LANES), jnp.bfloat16)
    is_early = lax.broadcasted_iota(jnp.int32, (IN_DEV, LANES), 1) < CH_DEV * (TAPS - 1)
    copies = []
    for block in range(BLOCKS):
        picked = picked_ref[block]
        values = [[none] * 8, [none] * 8]
        for parity in range(2):
            lanes = slice(parity * LANES, (parity + 1) * LANES)
            early = calibrate(
                z_ref[parity], t_ref[block, parity], picked[0:16, lanes], picked[16:32, lanes]
            )
            for part in range(2):
                for f in range(TAPS - 1):
                    values[part][2 * f + parity] = early[part][f].astype(jnp.bfloat16)
        for part in range(2):
            arrays = swap_groups(values[part])
            for d in range(32):
                rows = pl.ds((block * 32 + d) * IN_DEV, IN_DEV)
                lanes = pl.ds(part * LANES, LANES)
                moved = arrays[d % 8]
                if d >= 8:
                    moved = pltpu.roll(moved, LANES - 32 * (d // 8), 1)
                out_ref[rows, lanes] = jnp.where(is_early, moved, later_ref[rows, lanes])
        rows = pl.ds(block * 32 * IN_DEV, 32 * IN_DEV)
        copies.append(pltpu.make_async_copy(out_ref.at[rows], out_hbm.at[rows], sems.at[block]))
        copies[block].start()
    for copy in copies:
        copy.wait()


IN_VMEM = pl.BlockSpec(memory_space=pltpu.VMEM)
IN_HBM = pl.BlockSpec(memory_space=pltpu.HBM)


def channelize_later(samples, gains):
    table = folded_table()
    return pl.pallas_call(
        later_kernel,
        in_specs=[IN_HBM] * 5,
        out_specs=[IN_VMEM] * 5,
        out_shape=[
            pltpu.VMEM((IN_DEV, F_DEV * FRAME), jnp.bfloat16),
            pltpu.VMEM((TAPS, FRAME), jnp.float32),
            pltpu.VMEM(table.shape, jnp.bfloat16),
            pltpu.VMEM((INPUTS, 256), jnp.bfloat16),
            pltpu.VMEM((BLOCKS, 2 * IN_DEV, 2 * LANES), jnp.float32),
        ],
        scratch_shapes=[
            pltpu.VMEM((256, 256), jnp.bfloat16),
            pltpu.VMEM((2, IN_DEV, CHANNELS), jnp.float32),
            pltpu.VMEM((2, LATER * IN_DEV, HALF), jnp.bfloat16),
            pltpu.SemaphoreType.DMA((4 + BLOCKS,)),
        ],
        compiler_params=pltpu.CompilerParams(vmem_limit_bytes=ALL_VMEM),
        cost_estimate=pl.CostEstimate(
            flops=2 * 256 * 1024 * 2048, bytes_accessed=7 * 1024 * 1024, transcendentals=0
        ),
        name="channelize_later",
    )(
        *(
            pltpu.with_memory_space_constraint(x, pltpu.HBM)
            for x in (
                samples,
                jnp.asarray(pfb_window()),
                jnp.asarray(table),
                jnp.asarray(gain_select()),
                gains,
            )
        )
    )


def channelize_first(samples, prior, window, table, picked, later):
    return pl.pallas_call(
        first_kernel,
        in_specs=[IN_VMEM] * 6,
        out_specs=IN_HBM,
        out_shape=jax.ShapeDtypeStruct((INPUTS, 256), jnp.bfloat16),
        scratch_shapes=[
            pltpu.VMEM((2, (TAPS - 1) * IN_DEV, HALF), jnp.bfloat16),
            pltpu.VMEM((INPUTS, 256), jnp.bfloat16),
            pltpu.SemaphoreType.DMA((BLOCKS,)),
        ],
        compiler_params=pltpu.CompilerParams(vmem_limit_bytes=BEAM_VMEM),
        cost_estimate=pl.CostEstimate(
            flops=2 * 48 * 1024 * 2048, bytes_accessed=7 * 1024 * 1024, transcendentals=0
        ),
        name="channelize_first",
    )(samples, prior, window, table, picked, later)


def one_hot_kernel(slots_ref, order_ref, ids_ref, head_ref, rest_hbm, turn_hbm, rest_ref, turn_ref, sems):
    slots = jnp.transpose(slots_ref[...])
    copies = []
    for block in [*range(HEAD // LANES), *range(MADE // LANES, INPUTS // LANES)]:
        hot = jnp.where(slots[:, block : block + 1] == ids_ref[...], 1.0, 0.0).astype(jnp.bfloat16)
        at = block * LANES
        if at < HEAD:
            head_ref[pl.ds(at, LANES), :] = hot
            continue
        rows = pl.ds(at - MADE, LANES)
        rest_ref[rows, :] = hot
        copies.append(
            pltpu.make_async_copy(rest_ref.at[rows], rest_hbm.at[rows], sems.at[len(copies)])
        )
        copies[-1].start()
    beams = jnp.transpose(order_ref[...])
    index = lax.broadcasted_iota(jnp.int32, (2 * CH_DEV, BEAMS), 1)
    for pair in range(BEAMS // (2 * CH_DEV)):
        columns = []
        for g in RING[2 * pair : 2 * pair + 2]:
            row = g * CH_DEV % LANES
            at = g * CH_DEV // LANES
            columns.append(beams[row : row + CH_DEV, at : at + 1])
        turn_ref[pl.ds(pair * 2 * CH_DEV, 2 * CH_DEV), :] = jnp.where(
            jnp.concatenate(columns, 0) == index, 1.0, 0.0
        ).astype(jnp.bfloat16)
    copies.append(pltpu.make_async_copy(turn_ref, turn_hbm, sems.at[len(copies)]))
    copies[-1].start()
    for copy in copies:
        copy.wait()


def one_hots(slots, beam_order, ids):
    return pl.pallas_call(
        one_hot_kernel,
        in_specs=[IN_VMEM] * 3,
        out_specs=[IN_VMEM, IN_HBM, IN_HBM],
        out_shape=[
            pltpu.VMEM((HEAD, INPUTS), jnp.bfloat16),
            pltpu.HBM((INPUTS - MADE, INPUTS), jnp.bfloat16),
            pltpu.HBM((BEAMS, BEAMS), jnp.bfloat16),
        ],
        scratch_shapes=[
            pltpu.VMEM((INPUTS - MADE, INPUTS), jnp.bfloat16),
            pltpu.VMEM((BEAMS, BEAMS), jnp.bfloat16),
            pltpu.SemaphoreType.DMA(((INPUTS - MADE) // LANES + 1,)),
        ],
        compiler_params=pltpu.CompilerParams(vmem_limit_bytes=BEAM_VMEM),
        cost_estimate=pl.CostEstimate(
            flops=20 * 1024 * 1024, bytes_accessed=10 * 1024 * 1024, transcendentals=0
        ),
        name="one_hots",
    )(
        slots,
        beam_order.reshape(BEAMS // LANES, LANES),
        ids,
    )


def beam_kernel(
    x_ref,
    head_ref,
    rest_hbm,
    turn_hbm,
    north_ref,
    fine_ref,
    slots_ref,
    ids_ref,
    out_ref,
    made_ref,
    rest_ref,
    turn_ref,
    fed_ref,
    north_out_ref,
    beam_ref,
    power_ref,
    total_ref,
    sems,
):
    rest_copy = pltpu.make_async_copy(rest_hbm, rest_ref, sems.at[0])
    turn_copy = pltpu.make_async_copy(turn_hbm, turn_ref, sems.at[1])
    rest_copy.start()
    turn_copy.start()
    slots = jnp.transpose(slots_ref[...])
    def feed(step):
        at = step * FEEDS
        if at < HEAD:
            pick = head_ref[pl.ds(at, FEEDS), :]
        elif at < MADE:
            for block in range(at // LANES, (at + FEEDS) // LANES):
                made_ref[pl.ds(block * LANES - HEAD, LANES), :] = jnp.where(
                    slots[:, block : block + 1] == ids_ref[...], 1.0, 0.0
                ).astype(jnp.bfloat16)
            pick = made_ref[pl.ds(at - HEAD, FEEDS), :]
        else:
            if at == MADE:
                rest_copy.wait()
            pick = rest_ref[pl.ds(at - MADE, FEEDS), :]
        fed_ref[pl.ds(at, FEEDS), :] = jnp.dot(
            pick, x_ref[...], preferred_element_type=jnp.float32
        ).astype(jnp.bfloat16)

    def north(step):
        rows = pl.ds(step * FEEDS, FEEDS)
        both = jnp.dot(north_ref[...], fed_ref[rows, :], preferred_element_type=jnp.float32)
        north_out_ref[step, 0] = both[:FEEDS, :LANES] + both[FEEDS:, LANES:]
        north_out_ref[step, 1] = both[:FEEDS, LANES:] - both[FEEDS:, :LANES]

    def east(pol, row):
        rows = pl.ds(row, ROWS)
        re = [north_out_ref[pol * CYL + c, 0, rows, :] for c in range(CYL)]
        im = [north_out_ref[pol * CYL + c, 1, rows, :] for c in range(CYL)]
        sum_re, dif_re = re[0] + re[2], re[0] - re[2]
        sum_im, dif_im = im[0] + im[2], im[0] - im[2]
        odd_re, odd_dif_re = re[1] + re[3], re[1] - re[3]
        odd_im, odd_dif_im = im[1] + im[3], im[1] - im[3]
        out = (
            (sum_re + odd_re, sum_im + odd_im),
            (dif_re + odd_dif_im, dif_im - odd_dif_re),
            (sum_re - odd_re, sum_im - odd_im),
            (dif_re - odd_dif_im, dif_im + odd_dif_re),
        )
        for e in range(CYL):
            at = pl.ds(e * FEEDS + row, ROWS)
            beam_ref[at, :LANES] = out[e][0].astype(jnp.bfloat16)
            beam_ref[at, LANES:] = out[e][1].astype(jnp.bfloat16)

    def detect(pol, e):
        rows = pl.ds(e * FEEDS, FEEDS)
        fine = jnp.dot(beam_ref[rows, :], fine_ref[...], preferred_element_type=jnp.float32)
        squares = fine * fine
        power = squares[:, :LANES] + squares[:, LANES:]
        if pol == 0:
            power_ref[rows, :] = power
        else:
            total_ref[rows, :] = (0.25 * (power_ref[rows, :] + power)).astype(jnp.bfloat16)

    for pol in range(POLS):
        for cyl in range(CYL):
            feed(pol * CYL + cyl)
        for cyl in range(CYL):
            north(pol * CYL + cyl)
        for row in range(0, FEEDS, ROWS):
            east(pol, row)
        for e in range(CYL):
            detect(pol, e)
    turn_copy.wait()
    out_ref[...] = jnp.dot(
        turn_ref[...], total_ref[...], preferred_element_type=jnp.float32
    ).astype(jnp.bfloat16)


def form_beams(piece, head, rest, turn, slots, ids):
    return pl.pallas_call(
        beam_kernel,
        in_specs=[IN_VMEM, IN_VMEM, IN_HBM, IN_HBM, IN_VMEM, IN_VMEM, IN_VMEM, IN_VMEM],
        out_specs=IN_VMEM,
        out_shape=jax.ShapeDtypeStruct((BEAMS, LANES), jnp.bfloat16),
        scratch_shapes=[
            pltpu.VMEM((MADE - HEAD, INPUTS), jnp.bfloat16),
            pltpu.VMEM((INPUTS - MADE, INPUTS), jnp.bfloat16),
            pltpu.VMEM((BEAMS, BEAMS), jnp.bfloat16),
            pltpu.VMEM((INPUTS, 256), jnp.bfloat16),
            pltpu.VMEM((POLS * CYL, 2, FEEDS, LANES), jnp.float32),
            pltpu.VMEM((BEAMS, 256), jnp.bfloat16),
            pltpu.VMEM((BEAMS, LANES), jnp.float32),
            pltpu.VMEM((BEAMS, LANES), jnp.bfloat16),
            pltpu.SemaphoreType.DMA((2,)),
        ],
        compiler_params=pltpu.CompilerParams(vmem_limit_bytes=BEAM_VMEM),
        cost_estimate=pl.CostEstimate(
            flops=2 * 1024 * 1024 * 1500, bytes_accessed=12 * 1024 * 1024, transcendentals=0
        ),
        name="form_beams",
    )(
        piece,
        head,
        pltpu.with_memory_space_constraint(rest, pltpu.HBM),
        pltpu.with_memory_space_constraint(turn, pltpu.HBM),
        jnp.asarray(north_table()),
        jnp.asarray(fine_table()),
        slots,
        ids,
    )


def widen_kernel(x_ref, out_ref):
    for g in range(CHANNELS // CH_DEV):
        out_ref[0, :, g * LANES : (g + 1) * LANES] = x_ref[g].astype(jnp.float32)


def widen(power):
    slots = power.shape[0] * CH_DEV // CHANNELS
    return pl.pallas_call(
        widen_kernel,
        out_shape=jax.ShapeDtypeStruct((1, slots, CHANNELS * UPCH), jnp.float32),
        compiler_params=pltpu.CompilerParams(vmem_limit_bytes=BEAM_VMEM),
        name="widen",
    )(power.reshape(CHANNELS // CH_DEV, slots, LANES))


def body(samples, gains, slot_inputs, beam_order):
    tail = samples[:, (F_DEV - TAPS + 1) * FRAME :]
    prior = from_behind(tail, "ta", 1)
    held, window, table, later, picked = channelize_later(samples, gains)
    calibrated = channelize_first(held, prior, window, table, picked, later)
    piece = exchange(calibrated)
    ids = np.concatenate([np.arange(g * IN_DEV, (g + 1) * IN_DEV) for g in RING])
    ids = jnp.asarray(ids[None, :], jnp.int32)
    slots = slot_inputs.reshape(INPUTS // LANES, LANES)
    head, rest, turn = one_hots(slots, beam_order, ids)
    power = form_beams(piece, head, rest, turn, slots, ids)
    owned = exchange(power)
    return widen(owned)


def solution(mesh):
    placed = (P("gx", "ta"), P(None, "gx", None), P(), P())
    return jax.shard_map(
        body, mesh=mesh, in_specs=placed, out_specs=P("ta", "gx", None), check_vma=False
    )
```
